32 devices in a mesh: mem: 2 (over core), grid: 16 (over z, y, x).
Axes of the slice: x: 2, y: 2, z: 4, core: 2. Of those that a mesh axis runs over, the one named last changes fastest.
Arguments:
- control: bfloat16 [8, 32, 368, 736], P('mem', None, 'grid'), may hold values from -6 to 6
- perturbation: bfloat16 [8, 32, 736, 368], P('mem', None, 'grid'), may hold values from -6 to 6
- vertical: bfloat16 [32, 32], replicated, may hold values from 0 to 1
- lat_counts: int32 [16], replicated, may hold values from 1 to 23, 361 in all
- lon_counts: int32 [16], replicated, may hold values from 1 to 46, 720 in all
Outputs:
- increment: float32 [32, 736, 368], P('mem', 'grid')
The draws below stay inside these ranges and needn't reach their ends.
Inputs may be any that keep to these rules, and one draw needn't show every extreme that they name: Slab g holds its first lat_counts[g] latitude slots as real rows, numbered on from the slabs before it. Slab g holds its first lon_counts[g] longitude slots as real columns, numbered on from the slabs before it.
All inputs are finite; a program needn't handle non-finite values.
Results may differ from the reference program's by a relative error of at most 0.0067.
Values may be sent and summed in bfloat16 or wider, within the bound.
No kernel may reach another device: no remote copies, remote signals or barrier semaphores. Data moves between devices by JAX's collectives and lax.ppermute only.
A program may use at most 128 MiB of HBM per device.

```python
import math
import jax
import jax.numpy as jnp
import numpy as np
from jax import lax

LAT = 361
LON = 720
LEV = 32
LENGTH = 8
BAND = 48
MEMBERS = 8
LAT_SLOT = 23
LON_SLOT = 46
LAT_PAD = 368
LON_PAD = 736
N_GRID = 16


def draw_vertical(key, part):
    level_index = jnp.arange(LEV).astype(jnp.float32)
    decay_base = jnp.exp(-jnp.abs(level_index[:, None] - level_index[None, :]) / 4.0)
    factor = jax.random.uniform(key, (LEV, LEV), jnp.float32, 0.5, 1.5)
    return (decay_base * factor / 3.0).astype(jnp.bfloat16)


def raised(array, own_key, source, target, shards_of, factor):
    owner, partner = [(jnp.arange(array.shape[dim]) // (array.shape[dim] // shards_of)).reshape([-1 if axis == dim else 1 for axis in range(array.ndim)]) for dim in (source, target)]
    chosen = jax.random.permutation(own_key, shards_of)[partner]
    strong = (owner == chosen) | (owner == (partner + shards_of // 2) % shards_of)
    return jnp.where(strong, factor * array, array)


def steps_of(key, dims, pieces, smallest, largest):
    level, own = 1.0, jax.random.fold_in(key, 6)
    for dim, blocks in pieces:
        draws = jnp.exp(jax.random.uniform(jax.random.fold_in(own, dim), (blocks,), jnp.float32, smallest / len(pieces), largest / len(pieces)))
        level = level * jnp.repeat(draws, dims[dim] // blocks).reshape([-1 if axis == dim else 1 for axis in range(len(dims))])
    return level


def profile(amount, total, reach, slope):
    loads = [(1 << 20) // math.isqrt(grade ** slope) + 1 for grade in range(2, amount + 1)]
    surplus, given = total - reach - (amount - 1), [1] * (amount - 1)
    while surplus > 0:
        movable = [i for i in range(amount - 1) if given[i] < reach]
        whole, remaining = sum([loads[i] for i in movable]), surplus
        for i in movable:
            more = min(reach - given[i], max(1, remaining * loads[i] // whole), surplus)
            given[i] = given[i] + more
            surplus = surplus - more
    return np.array([reach] + given)


def uneven(key, count, total, most, lean):
    if count == 2:
        one = jax.random.randint(key, (), max(1, total - most), min(most, total - 1) + 1)
        return jnp.stack([one, total - one])
    tallies = jnp.asarray(profile(count, total, most, lean), jnp.int32)
    couples = (count - 1) // 2
    source_of, receiver = tallies[1:1 + 2 * couples:2], tallies[2:2 + 2 * couples:2]
    margin = jnp.minimum(source_of - 1, most - receiver)
    shifted = jax.random.randint(jax.random.fold_in(key, 1), (couples,), 0, 1 << 20) % (margin + 1)
    tallies = tallies.at[1:1 + 2 * couples:2].set(source_of - shifted).at[2:2 + 2 * couples:2].set(receiver + shifted)
    return tallies[jax.random.permutation(jax.random.fold_in(key, 2), count)]


def bell_draw(stream_key, shape, width, limit, pieces=(), held_as=jnp.bfloat16):
    factor_of = steps_of(stream_key, shape, pieces, -0.22, 0.18) if pieces else 1.0
    entries = jax.random.normal(stream_key, shape, jnp.float32) * width * factor_of
    return jnp.minimum(jnp.maximum(entries, -limit), limit).astype(held_as)


def gaussian_with(own_key, shape, scale, reach, shards, heavy, held_as=jnp.bfloat16):
    values = scale * jax.random.normal(own_key, shape, jnp.float32)
    if shards:
        values = values * steps_of(own_key, shape, shards, -0.22, 0.18)
    return jnp.clip(raised(values, jax.random.fold_in(own_key, 3), *heavy), -reach, reach).astype(held_as)


def setup_inputs(seed: int = 0) -> dict:
    streams_of = jax.random.split(jax.random.key(seed), 6)
    return {
        "control": bell_draw(streams_of[0], (MEMBERS, LEV, LAT_PAD, LON_PAD), 1.0, 6.0, ((0, 2), (2, 16))),
        "perturbation": gaussian_with(streams_of[1], (MEMBERS, LEV, LON_PAD, LAT_PAD), 1.0, 6.0, ((0, 2), (2, 16)), (0, 1, 2, 2.0)),
        "vertical": draw_vertical(jax.random.fold_in(streams_of[5], 71), 0),
        "lat_counts": uneven(streams_of[3], N_GRID, LAT, LAT_SLOT, 2).astype(jnp.int32),
        "lon_counts": uneven(streams_of[4], N_GRID, LON, LON_SLOT, 2).astype(jnp.int32),
    }


def slot_table(counts, slot_count):
    devices = counts.shape[0]
    slot_ids = jnp.arange(devices * slot_count, dtype=jnp.int32)
    device_of = slot_ids // slot_count
    offset_in = slot_ids - device_of * slot_count
    offsets = (jnp.cumsum(counts) - counts).astype(jnp.int32)
    one_hot = device_of[:, None] == jnp.arange(devices, dtype=jnp.int32)[None, :]
    count_of = lax.optimization_barrier(jnp.sum(jnp.where(one_hot, counts[None, :], 0), axis=1)).astype(jnp.int32)
    start_of = lax.optimization_barrier(jnp.sum(jnp.where(one_hot, offsets[None, :], 0), axis=1)).astype(jnp.int32)
    return ((start_of + offset_in).astype(jnp.int32), offset_in < count_of)

def pass_matrix(counts, slot_count, extent, periodic):
    position, usable = slot_table(counts, slot_count)
    lag = (position[None, :] - position[:, None]).astype(jnp.int32)
    if periodic:
        lag = jnp.where(lag < 0, lag + extent, lag).astype(jnp.int32)
    steps_f = jnp.arange(0, BAND + 1).astype(jnp.float32)
    normal_sum = jnp.sqrt(jnp.sum(jnp.exp(-2.0 * steps_f / LENGTH)))
    lag_f = lag.astype(jnp.float32)
    inside = (lag >= 0) & (lag <= BAND) & usable[:, None] & usable[None, :]
    weight = jnp.where(inside, jnp.exp(-lag_f / LENGTH) / normal_sum, 0.0)
    return weight.astype(jnp.bfloat16)

def reference(control, perturbation, vertical, lat_counts, lon_counts):
    lon_matrix = pass_matrix(lon_counts, LON_SLOT, LON, True)
    lat_matrix = pass_matrix(lat_counts, LAT_SLOT, LAT, False)
    vertical_f = vertical.astype(jnp.float32)

    def member_step(running, member_pair):
        ctrl_member, pert_member = member_pair
        smooth = jnp.dot(ctrl_member.reshape(-1, LON_PAD), lon_matrix, preferred_element_type=jnp.float32)
        smooth = smooth.astype(jnp.bfloat16).reshape(LEV, LAT_PAD, LON_PAD)
        smooth = jnp.swapaxes(smooth, 1, 2)
        smooth = jnp.dot(smooth.reshape(-1, LAT_PAD), lat_matrix, preferred_element_type=jnp.float32)
        smooth = smooth.astype(jnp.bfloat16).reshape(LEV, LON_PAD, LAT_PAD)
        mixed = jnp.einsum('kl,lci->kci', vertical_f, smooth.astype(jnp.float32))
        return (running + mixed * pert_member.astype(jnp.float32), None)
    start = jnp.zeros((LEV, LON_PAD, LAT_PAD), jnp.float32)
    summed, unused = lax.scan(member_step, start, (control, perturbation))
    return summed
```

```python
import functools
import math

import jax
import jax.numpy as jnp
import numpy as np
from jax import lax
from jax.experimental import pallas as pl
from jax.experimental.pallas import tpu as pltpu
from jax.sharding import PartitionSpec as P

LAT = 361
LON = 720
LENGTH = 8
BAND = 48
FAR = 1 << 20
NORM = np.float32(math.sqrt(sum(math.exp(-2.0 * e / LENGTH) for e in range(BAND + 1))))
VMEM_LIMIT = 56 * 1024 * 1024
NT = (((1,), (1,)), ((), ()))
NN = (((1,), (0,)), ((), ()))


def round_up(value, multiple):
    return -(-value // multiple) * multiple


def positions(counts, groups, slab, slots):
    place = jnp.full_like(slots, FAR)
    start = jnp.int32(0)
    for g in range(groups):
        count = counts[g]
        offset = slots - g * slab
        here = (offset >= 0) & (offset < count)
        place = jnp.where(here, offset + start, place)
        start = start + count
    return place


def weights(lag, real):
    inside = (lag >= 0) & (lag <= BAND) & real
    value = jnp.exp(lag.astype(jnp.float32) * (-1.0 / LENGTH)) / NORM
    return jnp.where(inside, value, 0.0).astype(jnp.bfloat16)


def lon_kernel(groups, counts, control, out, table, rows, packed, arrived):
    members, row_slots, levels, lon_pad = control.shape
    lanes = members * levels
    col_slots = lon_pad // groups
    col_rows = table.shape[0] // groups

    def fetch(i):
        return pltpu.make_async_copy(control.at[:, i], rows.at[i], arrived.at[i])

    for i in range(row_slots):
        fetch(i).start()

    source = positions(counts, groups, col_slots, lax.broadcasted_iota(jnp.int32, (1, lon_pad), 1))
    own = lax.broadcasted_iota(jnp.int32, (col_rows, 1), 0)
    start = jnp.int32(0)
    for g in range(groups):
        count = counts[g]
        lag = (own + start) - source
        lag = jnp.where(lag < 0, lag + LON, lag)
        table[g * col_rows:(g + 1) * col_rows, :] = weights(lag, own < count)
        start = start + count

    for i in range(row_slots):
        fetch(i).wait()
        field = rows[i].reshape(lanes, lon_pad)
        smooth = lax.dot_general(table[...], field, NT, preferred_element_type=jnp.float32)
        for g in range(groups):
            packed[g, i * col_slots:(i + 1) * col_slots, :] = smooth[g * col_rows:g * col_rows + col_slots]
    for g in range(groups):
        out[g] = packed[g].astype(jnp.bfloat16)


def lat_kernel(groups, row_slots, counts, member_group, mixer, received, pert, kept, given, table, field):
    members, col_slots, levels, lat_pad = pert.shape
    half = levels // 2
    useful = row_slots * col_slots
    second = member_group[0] == 1

    down = positions(counts, groups, row_slots, lax.broadcasted_iota(jnp.int32, (lat_pad, 1), 0))
    across = positions(counts, groups, row_slots, lax.broadcasted_iota(jnp.int32, (1, lat_pad), 1))
    table[...] = weights(down - across, down < FAR)
    for g in range(groups):
        field[g * useful:(g + 1) * useful, :] = received[g, :useful, :].astype(jnp.float32)

    def column(c, carry):
        part = field[pl.ds(c, lat_pad, col_slots), :].astype(jnp.bfloat16)
        smooth = lax.dot_general(table[...], part, NN, preferred_element_type=jnp.float32).astype(jnp.bfloat16)
        mixed = lax.dot_general(mixer[...], smooth, NT, preferred_element_type=jnp.float32)
        total = mixed[:levels] * pert[0, c].astype(jnp.float32)
        for m in range(1, members):
            total = total + mixed[m * levels:(m + 1) * levels] * pert[m, c].astype(jnp.float32)
        kept[c] = jnp.where(second, total[half:], total[:half])
        given[c] = jnp.where(second, total[:half], total[half:])
        return carry

    lax.fori_loop(0, col_slots, column, 0)


def per_device(control, perturbation, vertical, lat_counts, lon_counts):
    groups = lax.axis_size("grid")
    shares = lax.axis_size("mem")
    members, levels, row_slots, lon_pad = control.shape
    col_slots, lat_pad = perturbation.shape[2:]
    lanes = members * levels
    col_rows = round_up(col_slots, 8)
    sent_rows = round_up(row_slots * col_slots, 16)
    vmem = pl.BlockSpec(memory_space=pltpu.VMEM)
    smem = pl.BlockSpec(memory_space=pltpu.SMEM)
    params = pltpu.CompilerParams(vmem_limit_bytes=VMEM_LIMIT)

    smooth = pl.pallas_call(
        functools.partial(lon_kernel, groups),
        out_shape=jax.ShapeDtypeStruct((groups, sent_rows, lanes), jnp.bfloat16),
        in_specs=[smem, pl.BlockSpec(memory_space=pl.ANY)],
        out_specs=vmem,
        scratch_shapes=[
            pltpu.VMEM((groups * col_rows, lon_pad), jnp.bfloat16),
            pltpu.VMEM((row_slots, members, levels, lon_pad), jnp.bfloat16),
            pltpu.VMEM((groups, sent_rows, lanes), jnp.float32),
            pltpu.SemaphoreType.DMA((row_slots,)),
        ],
        compiler_params=params,
        name="lon_filter",
    )(lon_counts, jnp.transpose(control, (0, 2, 1, 3)))

    received = lax.all_to_all(smooth, "grid", split_axis=0, concat_axis=0, tiled=True)

    half = levels // 2
    member_group = (lax.axis_index("mem") if shares == 2 else jnp.int32(0)).reshape(1)
    mixer = jnp.kron(jnp.eye(members, dtype=jnp.bfloat16), vertical)

    shape = jax.ShapeDtypeStruct((col_slots, half, lat_pad), jnp.float32)
    kept, given = pl.pallas_call(
        functools.partial(lat_kernel, groups, row_slots),
        out_shape=(shape, shape),
        in_specs=[smem, smem, vmem, vmem, vmem],
        out_specs=(vmem, vmem),
        scratch_shapes=[
            pltpu.VMEM((lat_pad, lat_pad), jnp.bfloat16),
            pltpu.VMEM((lat_pad * col_slots, lanes), jnp.float32),
        ],
        compiler_params=params,
        name="lat_filter",
    )(lat_counts, member_group, mixer, received, jnp.transpose(perturbation, (0, 2, 1, 3)))
    if shares == 2:
        total = kept + lax.ppermute(given, "mem", [(0, 1), (1, 0)])
    else:
        total = lax.psum_scatter(
            jnp.concatenate([kept, given], axis=1), "mem", scatter_dimension=1, tiled=True
        )
    return jnp.transpose(total, (1, 0, 2))


def solution(mesh):
    in_specs = (P("mem", None, "grid", None), P("mem", None, "grid", None), P(), P(), P())
    out_specs = P("mem", "grid", None)
    return jax.shard_map(per_device, mesh=mesh, in_specs=in_specs, out_specs=out_specs, check_vma=False)
```

```python
import functools
import math

import jax
import jax.numpy as jnp
import numpy as np
from jax import lax
from jax.experimental import pallas as pl
from jax.experimental.pallas import tpu as pltpu
from jax.sharding import PartitionSpec as P

LAT = 361
LON = 720
LENGTH = 8
BAND = 48
FAR = 1 << 20
NORM = np.float32(math.sqrt(sum(math.exp(-2.0 * e / LENGTH) for e in range(BAND + 1))))
VMEM_LIMIT = 28 * 1024 * 1024
FIRST = 3
NT = (((1,), (1,)), ((), ()))
NN = (((1,), (0,)), ((), ()))


def round_up(value, multiple):
    return -(-value // multiple) * multiple


def sums_before(counts, starts, groups):
    total = jnp.int32(0)
    for g in range(groups):
        starts[g] = total
        total = total + counts[g]


def place_of(counts, starts, slab, slots, size):
    inside = (slots >= 0) & (slots < jnp.minimum(counts[slab], size))
    return jnp.where(inside, slots + starts[slab], FAR)


def weights(lag, real):
    inside = (lag >= 0) & (lag <= BAND) & real
    value = jnp.exp(lag.astype(jnp.float32) * (-1.0 / LENGTH)) / NORM
    return jnp.where(inside, value, 0.0).astype(jnp.bfloat16)


def lon_kernel(groups, masks, counts, me, control, *refs):
    outs, (table, rows, packed, starts, arrived) = refs[:len(masks)], refs[len(masks):]
    members, row_slots, levels, lon_pad = control.shape
    lanes = members * levels
    col_slots = lon_pad // groups
    col_rows = table.shape[0] // len(masks)

    def fetch(i):
        return pltpu.make_async_copy(control.at[:, i], rows.at[i], arrived.at[i])

    for i in range(row_slots):
        fetch(i).start()

    sums_before(counts, starts, groups)
    slots = lax.broadcasted_iota(jnp.int32, (1, lon_pad), 1)
    source = jnp.full_like(slots, FAR)
    for g in range(groups):
        source = jnp.minimum(source, place_of(counts, starts, g, slots - g * col_slots, col_slots))
    own = lax.broadcasted_iota(jnp.int32, (col_rows, 1), 0)
    for n, mask in enumerate(masks):
        slab = me[0] ^ mask
        lag = own + starts[slab] - source
        lag = jnp.where(lag < 0, lag + LON, lag)
        table[n * col_rows:(n + 1) * col_rows, :] = weights(lag, own < counts[slab])

    for i in range(0, row_slots, 2):
        count = min(2, row_slots - i)
        for r in range(count):
            fetch(i + r).wait()
        field = rows[i:i + count].reshape(count * lanes, lon_pad)
        smooth = lax.dot_general(table[...], field, NT, preferred_element_type=jnp.float32)
        for n in range(len(masks)):
            for r in range(count):
                packed[n, (i + r) * col_slots:(i + r + 1) * col_slots, :] = smooth[
                    n * col_rows:n * col_rows + col_slots, r * lanes:(r + 1) * lanes
                ]
    for n in range(len(masks)):
        outs[n][...] = packed[n].astype(jnp.bfloat16)


def lat_kernel(groups, row_slots, masks, counts, me, member_group, mixer, pert, *refs):
    received, (kept, given, table, field, starts) = refs[:groups], refs[groups:]
    members, col_slots, levels, lat_pad = pert.shape
    lanes = members * levels
    half = levels // 2
    useful = row_slots * col_slots
    second = member_group[0] == 1

    sums_before(counts, starts, groups)
    down_slots = lax.broadcasted_iota(jnp.int32, (lat_pad, 1), 0)
    across_slots = lax.broadcasted_iota(jnp.int32, (1, lat_pad), 1)
    down, across = jnp.full_like(down_slots, FAR), jnp.full_like(across_slots, FAR)
    for g in range(groups):
        down = jnp.minimum(down, place_of(counts, starts, g, down_slots - g * row_slots, row_slots))
        across = jnp.minimum(
            across, place_of(counts, starts, me[0] ^ masks[g], across_slots - g * row_slots, row_slots)
        )
    table[...] = weights(down - across, down < FAR)
    for g in range(groups):
        field[g * useful:(g + 1) * useful, :] = received[g][...].astype(jnp.float32)

    for c in range(0, col_slots, 2):
        part = jnp.concatenate(
            [field[pl.ds(c + r, lat_pad, col_slots), :].astype(jnp.bfloat16) for r in range(2)], axis=1
        )
        smooth = lax.dot_general(table[...], part, NN, preferred_element_type=jnp.float32).astype(jnp.bfloat16)
        for r in range(2):
            mixed = lax.dot_general(
                mixer[...], smooth[:, r * lanes:(r + 1) * lanes], NT, preferred_element_type=jnp.float32
            )
            total = mixed[:levels] * pert[0, c + r].astype(jnp.float32)
            for m in range(1, members):
                total = total + mixed[m * levels:(m + 1) * levels] * pert[m, c + r].astype(jnp.float32)
            kept[c + r] = jnp.where(second, total[half:], total[:half])
            given[c + r] = jnp.where(second, total[:half], total[half:])


def sending_order(groups):
    far = list(range(groups // 2, groups))
    near = list(range(groups // 4, groups // 2)) + list(range(1, groups // 4))
    order = []
    for n in range(groups // 2):
        order += far[n:n + 1] + near[n:n + 1]
    return order


def per_device(control, perturbation, vertical, lat_counts, lon_counts):
    groups = lax.axis_size("grid")
    shares = lax.axis_size("mem")
    members, levels, row_slots, lon_pad = control.shape
    col_slots, lat_pad = perturbation.shape[2:]
    lanes = members * levels
    col_rows = round_up(col_slots, 8)
    useful = row_slots * col_slots
    vmem = pl.BlockSpec(memory_space=pltpu.VMEM)
    smem = pl.BlockSpec(memory_space=pltpu.SMEM)
    params = pltpu.CompilerParams(vmem_limit_bytes=VMEM_LIMIT)
    me = lax.axis_index("grid").reshape(1)
    order = sending_order(groups)
    fields = jnp.transpose(control, (0, 2, 1, 3))

    def lon_filter(masks):
        return pl.pallas_call(
            functools.partial(lon_kernel, groups, masks),
            out_shape=[jax.ShapeDtypeStruct((useful, lanes), jnp.bfloat16)] * len(masks),
            in_specs=[smem, smem, pl.BlockSpec(memory_space=pl.ANY)],
            out_specs=[vmem] * len(masks),
            scratch_shapes=[
                pltpu.VMEM((len(masks) * col_rows, lon_pad), jnp.bfloat16),
                pltpu.VMEM((row_slots, members, levels, lon_pad), jnp.bfloat16),
                pltpu.VMEM((len(masks), useful, lanes), jnp.float32),
                pltpu.SMEM((groups,), jnp.int32),
                pltpu.SemaphoreType.DMA((row_slots,)),
            ],
            compiler_params=params,
            cost_estimate=pl.CostEstimate(
                flops=2 * len(masks) * col_rows * lon_pad * row_slots * lanes,
                bytes_accessed=2 * (lanes * row_slots * lon_pad + len(masks) * useful * lanes),
                transcendentals=0,
            ),
            name="lon_filter",
        )(lon_counts, me, fields)

    def send(mask, block):
        return lax.ppermute(block, "grid", [(g, g ^ mask) for g in range(groups)])

    first, rest = order[:FIRST], order[FIRST:] + [0]
    received = [send(mask, block) for mask, block in zip(first, lon_filter(first))]
    received += [send(mask, block) if mask else block for mask, block in zip(rest, lon_filter(rest))]
    masks = first + rest

    half = levels // 2
    member_group = (lax.axis_index("mem") if shares == 2 else jnp.int32(0)).reshape(1)
    mixer = jnp.kron(jnp.eye(members, dtype=jnp.bfloat16), vertical)

    shape = jax.ShapeDtypeStruct((col_slots, half, lat_pad), jnp.float32)
    kept, given = pl.pallas_call(
        functools.partial(lat_kernel, groups, row_slots, masks),
        out_shape=(shape, shape),
        in_specs=[smem, smem, smem] + [vmem] * (2 + groups),
        out_specs=(vmem, vmem),
        scratch_shapes=[
            pltpu.VMEM((lat_pad, lat_pad), jnp.bfloat16),
            pltpu.VMEM((lat_pad * col_slots, lanes), jnp.float32),
            pltpu.SMEM((groups,), jnp.int32),
        ],
        compiler_params=params,
        name="lat_filter",
    )(lat_counts, me, member_group, mixer, jnp.transpose(perturbation, (0, 2, 1, 3)), *received)
    if shares == 2:
        total = kept + lax.ppermute(given, "mem", [(0, 1), (1, 0)])
    else:
        total = lax.psum_scatter(
            jnp.concatenate([kept, given], axis=1), "mem", scatter_dimension=1, tiled=True
        )
    return jnp.transpose(total, (1, 0, 2))


def solution(mesh):
    in_specs = (P("mem", None, "grid", None), P("mem", None, "grid", None), P(), P(), P())
    out_specs = P("mem", "grid", None)
    return jax.shard_map(per_device, mesh=mesh, in_specs=in_specs, out_specs=out_specs, check_vma=False)
```

```python
import functools
import math

import jax
import jax.numpy as jnp
import numpy as np
from jax import lax
from jax.experimental import pallas as pl
from jax.experimental.pallas import tpu as pltpu
from jax.sharding import PartitionSpec as P

LAT = 361
LON = 720
LENGTH = 8
BAND = 48
FAR = 1 << 20
NORM = np.float32(math.sqrt(sum(math.exp(-2.0 * e / LENGTH) for e in range(BAND + 1))))
MIB = 1024 * 1024
LON_LIMIT = 24 * MIB
LAT_LIMIT = 26 * MIB
FIRST = 3
NT = (((1,), (1,)), ((), ()))
NN = (((1,), (0,)), ((), ()))


def round_up(value, multiple):
    return -(-value // multiple) * multiple


def sums_before(meta, first, starts, groups):
    total = jnp.int32(0)
    for g in range(groups):
        starts[g] = total
        total = total + meta[first + g]


def place_of(meta, first, starts, slab, slots, size):
    inside = (slots >= 0) & (slots < jnp.minimum(meta[first + slab], size))
    return jnp.where(inside, slots + starts[slab], FAR)


def weights(lag, real):
    inside = (lag >= 0) & (lag <= BAND) & real
    value = jnp.exp(lag.astype(jnp.float32) * (-1.0 / LENGTH)) / NORM
    return jnp.where(inside, value, 0.0).astype(jnp.bfloat16)


def lon_weights(groups, masks, meta, starts, table):
    lon_pad = table.shape[1]
    col_slots = lon_pad // groups
    col_rows = table.shape[0] // len(masks)
    sums_before(meta, 0, starts, groups)
    slots = lax.broadcasted_iota(jnp.int32, (1, lon_pad), 1)
    source = jnp.full_like(slots, FAR)
    for g in range(groups):
        source = jnp.minimum(source, place_of(meta, 0, starts, g, slots - g * col_slots, col_slots))
    own = lax.broadcasted_iota(jnp.int32, (col_rows, 1), 0)
    for n, mask in enumerate(masks):
        slab = meta[2 * groups] ^ mask
        lag = own + starts[slab] - source
        lag = jnp.where(lag < 0, lag + LON, lag)
        table[n * col_rows:(n + 1) * col_rows, :] = weights(lag, own < meta[slab])


def lon_kernel(groups, masks, meta, control, *refs):
    outs, (table, packed, starts) = refs[-3 - len(masks):-3], refs[-3:]
    members, row_slots, levels, lon_pad = control.shape
    lanes = members * levels
    col_slots = lon_pad // groups
    col_rows = table.shape[0] // len(masks)
    lon_weights(groups, masks, meta, starts, table)
    for i in range(0, row_slots, 2):
        count = min(2, row_slots - i)
        field = jnp.concatenate([control[:, i + r].reshape(lanes, lon_pad) for r in range(count)], axis=0)
        smooth = lax.dot_general(table[...], field, NT, preferred_element_type=jnp.float32)
        for n in range(len(masks)):
            for r in range(count):
                packed[n, (i + r) * col_slots:(i + r + 1) * col_slots, :] = smooth[
                    n * col_rows:n * col_rows + col_slots, r * lanes:(r + 1) * lanes
                ]
    for n in range(len(masks)):
        outs[n][...] = packed[n].astype(jnp.bfloat16)


def lat_weights(groups, row_slots, masks, meta, starts, table):
    lat_pad = table.shape[0]
    sums_before(meta, groups, starts, groups)
    down_slots = lax.broadcasted_iota(jnp.int32, (lat_pad, 1), 0)
    across_slots = lax.broadcasted_iota(jnp.int32, (1, lat_pad), 1)
    down, across = jnp.full_like(down_slots, FAR), jnp.full_like(across_slots, FAR)
    for g in range(groups):
        down = jnp.minimum(down, place_of(meta, groups, starts, g, down_slots - g * row_slots, row_slots))
        across = jnp.minimum(
            across, place_of(meta, groups, starts, meta[2 * groups] ^ masks[g], across_slots - g * row_slots, row_slots)
        )
    table[...] = weights(down - across, down < FAR)


def lat_columns(low, second, mixer, pert, table, field, kept, given):
    columns, half = kept.shape[:2]
    members, _, levels, lat_pad = pert.shape
    lanes = members * levels
    for c in range(0, columns, 2):
        part = jnp.concatenate(
            [field[pl.ds(c + r, lat_pad, columns), :].astype(jnp.bfloat16) for r in range(2)], axis=1
        )
        smooth = lax.dot_general(table[...], part, NN, preferred_element_type=jnp.float32).astype(jnp.bfloat16)
        for r in range(2):
            mixed = lax.dot_general(
                mixer[...], smooth[:, r * lanes:(r + 1) * lanes], NT, preferred_element_type=jnp.float32
            )
            total = mixed[:levels] * pert[0, low + c + r].astype(jnp.float32)
            for m in range(1, members):
                total = total + mixed[m * levels:(m + 1) * levels] * pert[m, low + c + r].astype(jnp.float32)
            kept[c + r] = jnp.where(second, total[half:], total[:half])
            given[c + r] = jnp.where(second, total[:half], total[half:])


def block_diagonal(vertical, copies):
    levels = vertical.shape[0]
    size = copies * levels
    place = lax.broadcasted_iota(jnp.int32, (size, levels), 0) - lax.broadcasted_iota(jnp.int32, (size, levels), 1)
    spread = place == 0
    across, down = (lax.broadcasted_iota(jnp.int32, (size, size), dim) for dim in (1, 0))
    same = (across < levels) & (down < levels)
    for m in range(1, copies):
        spread = spread | (place == m * levels)
        low, high = m * levels, (m + 1) * levels
        same = same | ((across >= low) & (across < high) & (down >= low) & (down < high))
    spread = jnp.where(spread, 1.0, 0.0).astype(jnp.bfloat16)
    tall = lax.dot_general(spread, vertical, NN, preferred_element_type=jnp.float32).astype(jnp.bfloat16)
    wide = lax.dot_general(tall, spread, NT, preferred_element_type=jnp.float32)
    return jnp.where(same, wide, 0.0).astype(jnp.bfloat16)


def lat_kernel(groups, row_slots, masks, meta, vertical, pert, *refs):
    received, (kept, given, mixer, table, field, starts) = refs[:groups], refs[groups:]
    columns = kept.shape[0]
    useful = row_slots * columns
    mixer[...] = block_diagonal(vertical[...], pert.shape[0])
    lat_weights(groups, row_slots, masks, meta, starts, table)
    for g in range(groups):
        field[g * useful:(g + 1) * useful, :] = received[g][...].astype(jnp.float32)
    lat_columns(0, meta[2 * groups + 1] == 1, mixer, pert, table, field, kept, given)


def sending_order(groups):
    quarter = groups // 4
    far = list(range(2 * quarter, 4 * quarter))
    near = list(range(quarter, 2 * quarter)) + list(range(1, quarter))
    order = []
    for n in range(2 * quarter):
        order += far[n:n + 1] + near[n:n + 1]
    return order


def per_device(control, perturbation, vertical, lat_counts, lon_counts):
    groups = lax.axis_size("grid")
    shares = lax.axis_size("mem")
    members, levels, row_slots, lon_pad = control.shape
    col_slots, lat_pad = perturbation.shape[2:]
    lanes = members * levels
    vmem = pl.BlockSpec(memory_space=pltpu.VMEM)
    smem = pl.BlockSpec(memory_space=pltpu.SMEM)
    hbm = pl.BlockSpec(memory_space=pl.ANY)
    places = jnp.stack([lax.axis_index("grid"), lax.axis_index("mem") if shares == 2 else 0]).astype(jnp.int32)
    meta = jnp.concatenate([lon_counts, lat_counts, places])
    pert = jnp.transpose(perturbation, (0, 2, 1, 3))

    fields = jnp.transpose(control, (0, 2, 1, 3))

    def lon_filter(masks, after):
        return list(pl.pallas_call(
            functools.partial(lon_kernel, groups, masks),
            out_shape=[jax.ShapeDtypeStruct((row_slots * col_slots, lanes), jnp.bfloat16)] * len(masks),
            in_specs=[smem, vmem] + [hbm] * len(after),
            out_specs=[vmem] * len(masks),
            scratch_shapes=[
                pltpu.VMEM((len(masks) * round_up(col_slots, 16), lon_pad), jnp.bfloat16),
                pltpu.VMEM((len(masks), row_slots * col_slots, lanes), jnp.float32),
                pltpu.SMEM((groups,), jnp.int32),
            ],
            compiler_params=pltpu.CompilerParams(vmem_limit_bytes=LON_LIMIT),
            name="lon_filter",
        )(meta, fields, *after))

    def send(mask, value):
        return lax.ppermute(value, "grid", [(g, g ^ mask) for g in range(groups)])

    order = sending_order(groups)
    masks = order + [0]
    values = lon_filter(order[:FIRST], [])
    values += lon_filter(masks[FIRST:], values[:1])
    received = [send(mask, value) if mask else value for mask, value in zip(masks, values)]

    half = levels // 2
    kept, given = pl.pallas_call(
        functools.partial(lat_kernel, groups, row_slots, masks),
        out_shape=[jax.ShapeDtypeStruct((col_slots, half, lat_pad), jnp.float32)] * 2,
        in_specs=[smem] + [vmem] * (2 + groups),
        out_specs=[vmem] * 2,
        scratch_shapes=[
            pltpu.VMEM((lanes, lanes), jnp.bfloat16),
            pltpu.VMEM((lat_pad, lat_pad), jnp.bfloat16),
            pltpu.VMEM((lat_pad * col_slots, lanes), jnp.float32),
            pltpu.SMEM((groups,), jnp.int32),
        ],
        compiler_params=pltpu.CompilerParams(vmem_limit_bytes=LAT_LIMIT),
        name="lat_filter",
    )(meta, vertical, pert, *received)
    if shares == 2:
        total = kept + lax.ppermute(given, "mem", [(0, 1), (1, 0)])
    else:
        total = lax.psum_scatter(
            jnp.concatenate([kept, given], axis=1), "mem", scatter_dimension=1, tiled=True
        )
    return jnp.transpose(total, (1, 0, 2))


def solution(mesh):
    in_specs = (P("mem", None, "grid", None), P("mem", None, "grid", None), P(), P(), P())
    out_specs = P("mem", "grid", None)
    return jax.shard_map(per_device, mesh=mesh, in_specs=in_specs, out_specs=out_specs, check_vma=False)
```

```python
import functools
import math

import jax
import jax.numpy as jnp
import numpy as np
from jax import lax
from jax.experimental import pallas as pl
from jax.experimental.pallas import tpu as pltpu
from jax.sharding import PartitionSpec as P

LAT = 361
LON = 720
LENGTH = 8
BAND = 48
FAR = 1 << 20
NORM = np.float32(math.sqrt(sum(math.exp(-2.0 * e / LENGTH) for e in range(BAND + 1))))
MIB = 1024 * 1024
LON_LIMIT = 24 * MIB
LAT_LIMIT = 26 * MIB
FIRST = 3
AHEAD = 2
NT = (((1,), (1,)), ((), ()))
NN = (((1,), (0,)), ((), ()))


def round_up(value, multiple):
    return -(-value // multiple) * multiple


def sums_before(meta, first, starts, groups):
    total = jnp.int32(0)
    for g in range(groups):
        starts[g] = total
        total = total + meta[first + g]


def place_of(meta, first, starts, slab, slots, size):
    inside = (slots >= 0) & (slots < jnp.minimum(meta[first + slab], size))
    return jnp.where(inside, slots + starts[slab], FAR)


def weights(lag, real):
    inside = (lag >= 0) & (lag <= BAND) & real
    value = jnp.exp(lag.astype(jnp.float32) * (-1.0 / LENGTH)) / NORM
    return jnp.where(inside, value, 0.0).astype(jnp.bfloat16)


def lon_weights(groups, masks, meta, starts, table):
    lon_pad = table.shape[1]
    col_slots = lon_pad // groups
    col_rows = table.shape[0] // len(masks)
    sums_before(meta, 0, starts, groups)
    slots = lax.broadcasted_iota(jnp.int32, (1, lon_pad), 1)
    source = jnp.full_like(slots, FAR)
    for g in range(groups):
        source = jnp.minimum(source, place_of(meta, 0, starts, g, slots - g * col_slots, col_slots))
    own = lax.broadcasted_iota(jnp.int32, (col_rows, 1), 0)
    for n, mask in enumerate(masks):
        slab = meta[2 * groups] ^ mask
        lag = own + starts[slab] - source
        lag = jnp.where(lag < 0, lag + LON, lag)
        table[n * col_rows:(n + 1) * col_rows, :] = weights(lag, own < meta[slab])


def lon_kernel(groups, masks, meta, control, *refs):
    outs, (table, packed, starts) = refs[-3 - len(masks):-3], refs[-3:]
    members, row_slots, levels, lon_pad = control.shape
    lanes = members * levels
    col_slots = lon_pad // groups
    col_rows = table.shape[0] // len(masks)
    lon_weights(groups, masks, meta, starts, table)
    for i in range(0, row_slots, 2):
        count = min(2, row_slots - i)
        field = jnp.concatenate([control[:, i + r].reshape(lanes, lon_pad) for r in range(count)], axis=0)
        smooth = lax.dot_general(table[...], field, NT, preferred_element_type=jnp.float32)
        for n in range(len(masks)):
            for r in range(count):
                packed[n, (i + r) * col_slots:(i + r + 1) * col_slots, :] = smooth[
                    n * col_rows:n * col_rows + col_slots, r * lanes:(r + 1) * lanes
                ]
    for n in range(len(masks)):
        outs[n][...] = packed[n].astype(jnp.bfloat16)


def lat_weights(groups, row_slots, masks, meta, starts, table):
    lat_pad = table.shape[0]
    sums_before(meta, groups, starts, groups)
    down_slots = lax.broadcasted_iota(jnp.int32, (lat_pad, 1), 0)
    across_slots = lax.broadcasted_iota(jnp.int32, (1, lat_pad), 1)
    down, across = jnp.full_like(down_slots, FAR), jnp.full_like(across_slots, FAR)
    for g in range(groups):
        down = jnp.minimum(down, place_of(meta, groups, starts, g, down_slots - g * row_slots, row_slots))
        across = jnp.minimum(
            across, place_of(meta, groups, starts, meta[2 * groups] ^ masks[g], across_slots - g * row_slots, row_slots)
        )
    table[...] = weights(down - across, down < FAR)


def lat_columns(second, mixer, pert, table, field, kept, given):
    columns, half = kept.shape[:2]
    members, _, levels, lat_pad = pert.shape
    lanes = members * levels

    def filtered(c):
        part = jnp.concatenate(
            [field[pl.ds(c + r, lat_pad, columns), :].astype(jnp.bfloat16) for r in range(2)], axis=1
        )
        return lax.dot_general(table[...], part, NN, preferred_element_type=jnp.float32).astype(jnp.bfloat16)

    def finish(c, smooth):
        for r in range(2):
            mixed = lax.dot_general(
                mixer[...], smooth[:, r * lanes:(r + 1) * lanes], NT, preferred_element_type=jnp.float32
            )
            total = mixed[:levels] * pert[0, c + r].astype(jnp.float32)
            for m in range(1, members):
                total = total + mixed[m * levels:(m + 1) * levels] * pert[m, c + r].astype(jnp.float32)
            kept[c + r] = jnp.where(second, total[half:], total[:half])
            given[c + r] = jnp.where(second, total[:half], total[half:]).astype(given.dtype)

    ahead = []
    for c in range(0, columns, 2):
        ahead.append((c, filtered(c)))
        if len(ahead) > AHEAD:
            finish(*ahead.pop(0))
    for item in ahead:
        finish(*item)


def block_diagonal(vertical, copies):
    levels = vertical.shape[0]
    size = copies * levels
    place = lax.broadcasted_iota(jnp.int32, (size, levels), 0) - lax.broadcasted_iota(jnp.int32, (size, levels), 1)
    spread = place == 0
    across, down = (lax.broadcasted_iota(jnp.int32, (size, size), dim) for dim in (1, 0))
    same = (across < levels) & (down < levels)
    for m in range(1, copies):
        spread = spread | (place == m * levels)
        low, high = m * levels, (m + 1) * levels
        same = same | ((across >= low) & (across < high) & (down >= low) & (down < high))
    spread = jnp.where(spread, 1.0, 0.0).astype(jnp.bfloat16)
    tall = lax.dot_general(spread, vertical, NN, preferred_element_type=jnp.float32).astype(jnp.bfloat16)
    wide = lax.dot_general(tall, spread, NT, preferred_element_type=jnp.float32)
    return jnp.where(same, wide, 0.0).astype(jnp.bfloat16)


def matrices_kernel(groups, row_slots, masks, meta, vertical, after, mixer, table, starts):
    mixer[...] = block_diagonal(vertical[...], mixer.shape[0] // vertical.shape[0])
    lat_weights(groups, row_slots, masks, meta, starts, table)


def lat_kernel(groups, meta, mixer, table, pert, *refs):
    received, (kept, given, field) = refs[:groups], refs[groups:]
    useful = received[0].shape[0]
    for g in range(groups):
        field[g * useful:(g + 1) * useful, :] = received[g][...].astype(jnp.float32)
    lat_columns(meta[2 * groups + 1] == 1, mixer, pert, table, field, kept, given)


def sending_order(groups):
    quarter = groups // 4
    far = list(range(2 * quarter, 4 * quarter))
    near = list(range(quarter, 2 * quarter)) + list(range(1, quarter))
    order = []
    for n in range(2 * quarter):
        order += far[n:n + 1] + near[n:n + 1]
    return order


def per_device(control, perturbation, vertical, lat_counts, lon_counts):
    groups = lax.axis_size("grid")
    shares = lax.axis_size("mem")
    members, levels, row_slots, lon_pad = control.shape
    col_slots, lat_pad = perturbation.shape[2:]
    lanes = members * levels
    vmem = pl.BlockSpec(memory_space=pltpu.VMEM)
    smem = pl.BlockSpec(memory_space=pltpu.SMEM)
    hbm = pl.BlockSpec(memory_space=pl.ANY)
    places = jnp.stack([lax.axis_index("grid"), lax.axis_index("mem") if shares == 2 else 0]).astype(jnp.int32)
    meta = jnp.concatenate([lon_counts, lat_counts, places])
    pert = jnp.transpose(perturbation, (0, 2, 1, 3))

    fields = jnp.transpose(control, (0, 2, 1, 3))

    def lon_filter(masks, after):
        return list(pl.pallas_call(
            functools.partial(lon_kernel, groups, masks),
            out_shape=[jax.ShapeDtypeStruct((row_slots * col_slots, lanes), jnp.bfloat16)] * len(masks),
            in_specs=[smem, vmem] + [hbm] * len(after),
            out_specs=[vmem] * len(masks),
            scratch_shapes=[
                pltpu.VMEM((len(masks) * round_up(col_slots, 16), lon_pad), jnp.bfloat16),
                pltpu.VMEM((len(masks), row_slots * col_slots, lanes), jnp.float32),
                pltpu.SMEM((groups,), jnp.int32),
            ],
            compiler_params=pltpu.CompilerParams(vmem_limit_bytes=LON_LIMIT),
            name="lon_filter",
        )(meta, fields, *after))

    def send(mask, value):
        return lax.ppermute(value, "grid", [(g, g ^ mask) for g in range(groups)])

    order = sending_order(groups)
    masks = order + [0]
    values = lon_filter(order[:FIRST], [])
    values += lon_filter(masks[FIRST:], values[:1])
    received = [send(mask, value) if mask else value for mask, value in zip(masks, values)]

    mixer, table = pl.pallas_call(
        functools.partial(matrices_kernel, groups, row_slots, masks),
        out_shape=[
            jax.ShapeDtypeStruct((lanes, lanes), jnp.bfloat16),
            jax.ShapeDtypeStruct((lat_pad, lat_pad), jnp.bfloat16),
        ],
        in_specs=[smem, vmem, hbm],
        out_specs=[vmem] * 2,
        scratch_shapes=[pltpu.SMEM((groups,), jnp.int32)],
        compiler_params=pltpu.CompilerParams(vmem_limit_bytes=4 * MIB),
        name="matrices",
    )(meta, vertical, values[-1])

    half = levels // 2
    kept, given = pl.pallas_call(
        functools.partial(lat_kernel, groups),
        out_shape=[
            jax.ShapeDtypeStruct((col_slots, half, lat_pad), jnp.float32),
            jax.ShapeDtypeStruct((col_slots, half, lat_pad), jnp.bfloat16 if shares == 2 else jnp.float32),
        ],
        in_specs=[smem] + [vmem] * (3 + groups),
        out_specs=[vmem] * 2,
        scratch_shapes=[pltpu.VMEM((lat_pad * col_slots, lanes), jnp.float32)],
        compiler_params=pltpu.CompilerParams(vmem_limit_bytes=LAT_LIMIT),
        name="lat_filter",
    )(meta, mixer, table, pert, *received)
    if shares == 2:
        total = kept + lax.ppermute(given, "mem", [(0, 1), (1, 0)]).astype(jnp.float32)
    else:
        total = lax.psum_scatter(
            jnp.concatenate([kept, given], axis=1), "mem", scatter_dimension=1, tiled=True
        )
    return jnp.transpose(total, (1, 0, 2))


def solution(mesh):
    in_specs = (P("mem", None, "grid", None), P("mem", None, "grid", None), P(), P(), P())
    out_specs = P("mem", "grid", None)
    return jax.shard_map(per_device, mesh=mesh, in_specs=in_specs, out_specs=out_specs, check_vma=False)
```

```python
import functools
import math

import jax
import jax.numpy as jnp
import numpy as np
from jax import lax
from jax.experimental import pallas as pl
from jax.experimental.pallas import tpu as pltpu
from jax.sharding import PartitionSpec as P

LAT = 361
LON = 720
LENGTH = 8
BAND = 48
FAR = 1 << 20
NORM = np.float32(math.sqrt(sum(math.exp(-2.0 * e / LENGTH) for e in range(BAND + 1))))
MIB = 1024 * 1024
FIRST_LIMIT = 60 * MIB
LON_LIMIT = 24 * MIB
LAT_LIMIT = 26 * MIB
FETCH = 12
AHEAD = 2
NT = (((1,), (1,)), ((), ()))
NN = (((1,), (0,)), ((), ()))


def round_up(value, multiple):
    return -(-value // multiple) * multiple


def sums_before(meta, first, starts, groups):
    total = jnp.int32(0)
    for g in range(groups):
        starts[g] = total
        total = total + meta[first + g]


def place_of(meta, first, starts, slab, slots, size):
    inside = (slots >= 0) & (slots < jnp.minimum(meta[first + slab], size))
    return jnp.where(inside, slots + starts[slab], FAR)


def weights(lag, real):
    inside = (lag >= 0) & (lag <= BAND) & real
    value = jnp.exp(lag.astype(jnp.float32) * (-1.0 / LENGTH)) / NORM
    return jnp.where(inside, value, 0.0).astype(jnp.bfloat16)


def lon_weights(groups, masks, meta, me, starts, table, slots, col_slots):
    col_rows = table.shape[0] // len(masks)
    sums_before(meta, 0, starts, groups)
    source = jnp.full_like(slots, FAR)
    for g in range(groups):
        source = jnp.minimum(source, place_of(meta, 0, starts, g, slots - g * col_slots, col_slots))
    own = lax.broadcasted_iota(jnp.int32, (col_rows, 1), 0)
    for n, mask in enumerate(masks):
        slab = me ^ mask
        lag = own + starts[slab] - source
        lag = jnp.where(lag < 0, lag + LON, lag)
        table[n * col_rows:(n + 1) * col_rows, :] = weights(lag, own < meta[slab])


def lon_blocks(masks, row_range, col_slots, rows_of, table, packed, outs):
    lanes = packed.shape[2]
    col_rows = table.shape[0] // len(masks)
    for i in row_range[::2]:
        count = min(2, row_range[-1] + 1 - i)
        field = jnp.concatenate([rows_of(i + r).reshape(lanes, table.shape[1]) for r in range(count)], axis=0)
        smooth = lax.dot_general(table[...], field, NT, preferred_element_type=jnp.float32)
        for n in range(len(masks)):
            for r in range(count):
                packed[n, (i + r) * col_slots:(i + r + 1) * col_slots, :] = smooth[
                    n * col_rows:n * col_rows + col_slots, r * lanes:(r + 1) * lanes
                ]
    for n, out in enumerate(outs):
        out[...] = packed[n].astype(jnp.bfloat16)


def window_tiles(groups, lon_pad):
    col_slots = lon_pad // groups
    tiles = -(-lon_pad // 128)
    reach = -(-(BAND + lon_pad - LON) // col_slots)
    needed = (reach + 2) * col_slots + 127 + tiles * 128 - lon_pad
    return reach, min(-(-needed // 128), tiles)


def window_begin(groups, lon_pad, mask):
    pair = (lax.axis_index("grid") ^ mask) // 2 * 2
    reach, width = window_tiles(groups, lon_pad)
    return lax.rem(pair - reach + groups, groups) * (lon_pad // groups) // 128


def first_lon_kernel(groups, masks, row_slots, lon_pad, counts, *refs):
    width = window_tiles(groups, lon_pad)[1]
    window, outs, (table, packed, starts) = refs[:width], refs[width:-3], refs[-3:]
    col_slots = lon_pad // groups
    tiles = -(-lon_pad // 128)
    begin = window_begin(groups, lon_pad, masks[0])
    lane = lax.broadcasted_iota(jnp.int32, (1, 128), 1)
    slots = [lane + lax.rem(begin + j, tiles) * 128 for j in range(width)]
    step = pl.program_id(0)
    size = window[0].shape[1]

    @pl.when(step == 0)
    def _():
        lon_weights(
            groups, masks, counts, lax.axis_index("grid"), starts, table, jnp.concatenate(slots, axis=1), col_slots
        )

    for n in range(-(-row_slots // size)):
        @pl.when(step == n)
        def _():
            def rows_of(i):
                return jnp.concatenate(
                    [
                        jnp.where(slots[j] < lon_pad, window[j][:, i - n * size].reshape(-1, 128), jnp.bfloat16(0))
                        for j in range(width)
                    ],
                    axis=1,
                )

            last = n * size + size >= row_slots
            lon_blocks(
                masks, range(n * size, row_slots if last else n * size + size), col_slots, rows_of, table, packed,
                outs if last else [],
            )


def lon_kernel(groups, masks, meta, control, *refs):
    outs, (table, packed, starts) = refs[-3 - len(masks):-3], refs[-3:]
    lon_pad = control.shape[3]
    col_slots = lon_pad // groups
    slots = lax.broadcasted_iota(jnp.int32, (1, lon_pad), 1)
    lon_weights(groups, masks, meta, meta[2 * groups], starts, table, slots, col_slots)
    lon_blocks(masks, range(control.shape[1]), col_slots, lambda i: control[:, i], table, packed, outs)


def lat_weights(groups, row_slots, masks, meta, starts, table):
    lat_pad = table.shape[0]
    sums_before(meta, groups, starts, groups)
    down_slots = lax.broadcasted_iota(jnp.int32, (lat_pad, 1), 0)
    across_slots = lax.broadcasted_iota(jnp.int32, (1, lat_pad), 1)
    down, across = jnp.full_like(down_slots, FAR), jnp.full_like(across_slots, FAR)
    for g in range(groups):
        down = jnp.minimum(down, place_of(meta, groups, starts, g, down_slots - g * row_slots, row_slots))
        across = jnp.minimum(
            across, place_of(meta, groups, starts, meta[2 * groups] ^ masks[g], across_slots - g * row_slots, row_slots)
        )
    table[...] = weights(down - across, down < FAR)


def lat_columns(second, mixer, pert, table, field, kept, given):
    columns, half = kept.shape[:2]
    members, _, levels, lat_pad = pert.shape
    lanes = members * levels

    def filtered(c):
        part = jnp.concatenate(
            [field[pl.ds(c + r, lat_pad, columns), :].astype(jnp.bfloat16) for r in range(2)], axis=1
        )
        return lax.dot_general(table[...], part, NN, preferred_element_type=jnp.float32).astype(jnp.bfloat16)

    def finish(c, smooth):
        for r in range(2):
            mixed = lax.dot_general(
                mixer[...], smooth[:, r * lanes:(r + 1) * lanes], NT, preferred_element_type=jnp.float32
            )
            total = mixed[:levels] * pert[0, c + r].astype(jnp.float32)
            for m in range(1, members):
                total = total + mixed[m * levels:(m + 1) * levels] * pert[m, c + r].astype(jnp.float32)
            kept[c + r] = jnp.where(second, total[half:], total[:half])
            given[c + r] = jnp.where(second, total[:half], total[half:]).astype(given.dtype)

    ahead = []
    for c in range(0, columns, 2):
        ahead.append((c, filtered(c)))
        if len(ahead) > AHEAD:
            finish(*ahead.pop(0))
    for item in ahead:
        finish(*item)


def block_diagonal(vertical, copies):
    levels = vertical.shape[0]
    size = copies * levels
    place = lax.broadcasted_iota(jnp.int32, (size, levels), 0) - lax.broadcasted_iota(jnp.int32, (size, levels), 1)
    spread = place == 0
    across, down = (lax.broadcasted_iota(jnp.int32, (size, size), dim) for dim in (1, 0))
    same = (across < levels) & (down < levels)
    for m in range(1, copies):
        spread = spread | (place == m * levels)
        low, high = m * levels, (m + 1) * levels
        same = same | ((across >= low) & (across < high) & (down >= low) & (down < high))
    spread = jnp.where(spread, 1.0, 0.0).astype(jnp.bfloat16)
    tall = lax.dot_general(spread, vertical, NN, preferred_element_type=jnp.float32).astype(jnp.bfloat16)
    wide = lax.dot_general(tall, spread, NT, preferred_element_type=jnp.float32)
    return jnp.where(same, wide, 0.0).astype(jnp.bfloat16)


def matrices_kernel(groups, row_slots, masks, meta, vertical, after, mixer, table, starts):
    mixer[...] = block_diagonal(vertical[...], mixer.shape[0] // vertical.shape[0])
    lat_weights(groups, row_slots, masks, meta, starts, table)


def lat_kernel(groups, meta, mixer, table, pert, *refs):
    received, (kept, given, field) = refs[:groups], refs[groups:]
    useful = received[0].shape[0]
    for g in range(groups):
        field[g * useful:(g + 1) * useful, :] = received[g][...].astype(jnp.float32)
    lat_columns(meta[2 * groups + 1] == 1, mixer, pert, table, field, kept, given)


def sending_order(groups):
    quarter = groups // 4
    far = list(range(2 * quarter, 4 * quarter))
    near = list(range(quarter, 2 * quarter)) + list(range(1, quarter))
    order = []
    for n in range(2 * quarter):
        order += far[n:n + 1] + near[n:n + 1]
    order.remove(far[1])
    return far[:1] + far[1:2] + order[1:]


def per_device(control, perturbation, vertical, lat_counts, lon_counts):
    groups = lax.axis_size("grid")
    shares = lax.axis_size("mem")
    members, levels, row_slots, lon_pad = control.shape
    col_slots, lat_pad = perturbation.shape[2:]
    lanes = members * levels
    vmem = pl.BlockSpec(memory_space=pltpu.VMEM)
    smem = pl.BlockSpec(memory_space=pltpu.SMEM)
    hbm = pl.BlockSpec(memory_space=pl.ANY)
    places = jnp.stack([lax.axis_index("grid"), lax.axis_index("mem") if shares == 2 else 0]).astype(jnp.int32)
    meta = jnp.concatenate([lon_counts, lat_counts, places])
    pert = jnp.transpose(perturbation, (0, 2, 1, 3))

    fields = jnp.transpose(control, (0, 2, 1, 3))

    def lon_filter(kernel, masks, columns, limit, grid, in_specs, *operands):
        return list(pl.pallas_call(
            kernel,
            out_shape=[jax.ShapeDtypeStruct((row_slots * col_slots, lanes), jnp.bfloat16)] * len(masks),
            grid=grid,
            in_specs=[smem, *in_specs],
            out_specs=[vmem] * len(masks),
            scratch_shapes=[
                pltpu.VMEM((len(masks) * round_up(col_slots, 16), columns), jnp.bfloat16),
                pltpu.VMEM((len(masks), row_slots * col_slots, lanes), jnp.float32),
                pltpu.SMEM((groups,), jnp.int32),
            ],
            compiler_params=pltpu.CompilerParams(vmem_limit_bytes=limit),
            name="lon_filter",
        )(*operands))

    def send(mask, value):
        return lax.ppermute(value, "grid", [(g, g ^ mask) for g in range(groups)])

    order = sending_order(groups)
    masks = order + [0]
    width = window_tiles(groups, lon_pad)[1]
    tiles = -(-lon_pad // 128)
    rows = min(FETCH, row_slots)
    windows = [
        pl.BlockSpec(
            (members, rows, levels, 128),
            lambda n, j=j: (0, n, 0, lax.rem(window_begin(groups, lon_pad, masks[0]) + j, tiles)),
        )
        for j in range(width)
    ]
    kernel = functools.partial(first_lon_kernel, groups, masks[:2], row_slots, lon_pad)
    values = lon_filter(
        kernel, masks[:2], width * 128, FIRST_LIMIT, (-(-row_slots // rows),), windows, lon_counts, *[fields] * width
    )
    kernel = functools.partial(lon_kernel, groups, masks[2:])
    values += lon_filter(kernel, masks[2:], lon_pad, LON_LIMIT, (), [vmem, hbm], meta, fields, values[0])
    received = [send(mask, value) if mask else value for mask, value in zip(masks, values)]

    mixer, table = pl.pallas_call(
        functools.partial(matrices_kernel, groups, row_slots, masks),
        out_shape=[
            jax.ShapeDtypeStruct((lanes, lanes), jnp.bfloat16),
            jax.ShapeDtypeStruct((lat_pad, lat_pad), jnp.bfloat16),
        ],
        in_specs=[smem, vmem, hbm],
        out_specs=[vmem] * 2,
        scratch_shapes=[pltpu.SMEM((groups,), jnp.int32)],
        compiler_params=pltpu.CompilerParams(vmem_limit_bytes=4 * MIB),
        name="matrices",
    )(meta, vertical, values[-1])

    half = levels // 2
    kept, given = pl.pallas_call(
        functools.partial(lat_kernel, groups),
        out_shape=[
            jax.ShapeDtypeStruct((col_slots, half, lat_pad), jnp.float32),
            jax.ShapeDtypeStruct((col_slots, half, lat_pad), jnp.bfloat16 if shares == 2 else jnp.float32),
        ],
        in_specs=[smem] + [vmem] * (3 + groups),
        out_specs=[vmem] * 2,
        scratch_shapes=[pltpu.VMEM((lat_pad * col_slots, lanes), jnp.float32)],
        compiler_params=pltpu.CompilerParams(vmem_limit_bytes=LAT_LIMIT),
        name="lat_filter",
    )(meta, mixer, table, pert, *received)
    if shares == 2:
        total = kept + lax.ppermute(given, "mem", [(0, 1), (1, 0)]).astype(jnp.float32)
    else:
        total = lax.psum_scatter(
            jnp.concatenate([kept, given], axis=1), "mem", scatter_dimension=1, tiled=True
        )
    return jnp.transpose(total, (1, 0, 2))


def solution(mesh):
    in_specs = (P("mem", None, "grid", None), P("mem", None, "grid", None), P(), P(), P())
    out_specs = P("mem", "grid", None)
    return jax.shard_map(per_device, mesh=mesh, in_specs=in_specs, out_specs=out_specs, check_vma=False)
```

```python
import functools
import math

import jax
import jax.numpy as jnp
import numpy as np
from jax import lax
from jax.experimental import pallas as pl
from jax.experimental.pallas import tpu as pltpu
from jax.sharding import PartitionSpec as P

LAT = 361
LON = 720
LENGTH = 8
BAND = 48
FAR = 1 << 20
NORM = np.float32(math.sqrt(sum(math.exp(-2.0 * e / LENGTH) for e in range(BAND + 1))))
MIB = 1024 * 1024
FIRST_LIMIT = 60 * MIB
LON_LIMIT = 24 * MIB
LAT_LIMIT = 26 * MIB
FETCH = 12
AHEAD = 3
NT = (((1,), (1,)), ((), ()))
NN = (((1,), (0,)), ((), ()))


def round_up(value, multiple):
    return -(-value // multiple) * multiple


def sums_before(meta, first, starts, groups):
    total = jnp.int32(0)
    for g in range(groups):
        starts[g] = total
        total = total + meta[first + g]


def place_of(meta, first, starts, slab, slots, size):
    inside = (slots >= 0) & (slots < jnp.minimum(meta[first + slab], size))
    return jnp.where(inside, slots + starts[slab], FAR)


def weights(lag, real):
    inside = (lag >= 0) & (lag <= BAND) & real
    value = jnp.exp(lag.astype(jnp.float32) * (-1.0 / LENGTH)) / NORM
    return jnp.where(inside, value, 0.0).astype(jnp.bfloat16)


def lon_weights(groups, masks, meta, me, starts, table, slots, col_slots):
    col_rows = table.shape[0] // len(masks)
    sums_before(meta, 0, starts, groups)
    source = jnp.full_like(slots, FAR)
    for g in range(groups):
        source = jnp.minimum(source, place_of(meta, 0, starts, g, slots - g * col_slots, col_slots))
    own = lax.broadcasted_iota(jnp.int32, (col_rows, 1), 0)
    for n, mask in enumerate(masks):
        slab = me ^ mask
        lag = own + starts[slab] - source
        lag = jnp.where(lag < 0, lag + LON, lag)
        table[n * col_rows:(n + 1) * col_rows, :] = weights(lag, own < meta[slab])


def lon_blocks(masks, row_range, col_slots, rows_of, table, packed, outs):
    lanes = packed.shape[2]
    col_rows = table.shape[0] // len(masks)
    for i in row_range[::2]:
        count = min(2, row_range[-1] + 1 - i)
        field = jnp.concatenate([rows_of(i + r).reshape(lanes, table.shape[1]) for r in range(count)], axis=0)
        smooth = lax.dot_general(table[...], field, NT, preferred_element_type=jnp.float32)
        for n in range(len(masks)):
            for r in range(count):
                packed[n, (i + r) * col_slots:(i + r + 1) * col_slots, :] = smooth[
                    n * col_rows:n * col_rows + col_slots, r * lanes:(r + 1) * lanes
                ]
    for n, out in enumerate(outs):
        out[...] = packed[n].astype(jnp.bfloat16)


def window_tiles(groups, lon_pad):
    col_slots = lon_pad // groups
    tiles = -(-lon_pad // 128)
    reach = -(-(BAND + lon_pad - LON) // col_slots)
    needed = (reach + 2) * col_slots + 127 + tiles * 128 - lon_pad
    return reach, min(-(-needed // 128), tiles)


def window_begin(groups, lon_pad, mask):
    pair = (lax.axis_index("grid") ^ mask) // 2 * 2
    reach, width = window_tiles(groups, lon_pad)
    return lax.rem(pair - reach + groups, groups) * (lon_pad // groups) // 128


def first_lon_kernel(groups, masks, row_slots, lon_pad, counts, *refs):
    width = window_tiles(groups, lon_pad)[1]
    window, outs, (table, packed, starts) = refs[:width], refs[width:-3], refs[-3:]
    col_slots = lon_pad // groups
    tiles = -(-lon_pad // 128)
    begin = window_begin(groups, lon_pad, masks[0])
    lane = lax.broadcasted_iota(jnp.int32, (1, 128), 1)
    slots = [lane + lax.rem(begin + j, tiles) * 128 for j in range(width)]
    step = pl.program_id(0)
    size = window[0].shape[1]

    @pl.when(step == 0)
    def _():
        lon_weights(
            groups, masks, counts, lax.axis_index("grid"), starts, table, jnp.concatenate(slots, axis=1), col_slots
        )

    for n in range(-(-row_slots // size)):
        @pl.when(step == n)
        def _():
            def rows_of(i):
                return jnp.concatenate(
                    [
                        jnp.where(slots[j] < lon_pad, window[j][:, i - n * size].reshape(-1, 128), jnp.bfloat16(0))
                        for j in range(width)
                    ],
                    axis=1,
                )

            last = n * size + size >= row_slots
            lon_blocks(
                masks, range(n * size, row_slots if last else n * size + size), col_slots, rows_of, table, packed,
                outs if last else [],
            )


def lon_kernel(groups, masks, meta, control, *refs):
    outs, (table, packed, starts) = refs[-3 - len(masks):-3], refs[-3:]
    lon_pad = control.shape[3]
    col_slots = lon_pad // groups
    slots = lax.broadcasted_iota(jnp.int32, (1, lon_pad), 1)
    lon_weights(groups, masks, meta, meta[2 * groups], starts, table, slots, col_slots)
    lon_blocks(masks, range(control.shape[1]), col_slots, lambda i: control[:, i], table, packed, outs)


def lat_reach(groups, row_slots):
    return -(-(BAND + groups * row_slots - LAT) // row_slots)


def lat_weights(groups, row_slots, meta, starts, table, first_down, first_across):
    sums_before(meta, groups, starts, groups)
    down_slots = lax.broadcasted_iota(jnp.int32, (table.shape[0], 1), 0) + first_down
    across_slots = lax.broadcasted_iota(jnp.int32, (1, table.shape[1]), 1) + first_across
    down, across = jnp.full_like(down_slots, FAR), jnp.full_like(across_slots, FAR)
    for g in range(groups):
        down = jnp.minimum(down, place_of(meta, groups, starts, g, down_slots - g * row_slots, row_slots))
        across = jnp.minimum(across, place_of(meta, groups, starts, g, across_slots - g * row_slots, row_slots))
    table[...] = weights(down - across, down < FAR)


def lat_columns(second, mixer, pert, upper, lower, field, kept, given):
    columns, half = kept.shape[:2]
    members, _, levels, lat_pad = pert.shape
    lanes = members * levels

    def filtered(c):
        halves = []
        for table, first in ((upper, 0), (lower, lat_pad - lower.shape[1])):
            part = jnp.concatenate(
                [
                    field[pl.ds(first * columns + c + r, table.shape[1], columns), :].astype(jnp.bfloat16)
                    for r in range(2)
                ],
                axis=1,
            )
            halves.append(lax.dot_general(table[...], part, NN, preferred_element_type=jnp.float32))
        return jnp.concatenate(halves, axis=0).astype(jnp.bfloat16)

    def finish(c, smooth):
        pair = lax.dot_general(mixer[...], smooth, NT, preferred_element_type=jnp.float32)
        for r in range(2):
            mixed = pair[r * lanes:(r + 1) * lanes]
            total = mixed[:levels] * pert[0, c + r].astype(jnp.float32)
            for m in range(1, members):
                total = total + mixed[m * levels:(m + 1) * levels] * pert[m, c + r].astype(jnp.float32)
            kept[c + r] = jnp.where(second, total[half:], total[:half])
            given[c + r] = jnp.where(second, total[:half], total[half:]).astype(given.dtype)

    ahead = []
    for c in range(0, columns, 2):
        ahead.append((c, filtered(c)))
        if len(ahead) > AHEAD:
            finish(*ahead.pop(0))
    for item in ahead:
        finish(*item)


def block_diagonal(vertical, copies):
    levels = vertical.shape[0]
    size = copies * levels
    place = lax.broadcasted_iota(jnp.int32, (size, levels), 0) - lax.broadcasted_iota(jnp.int32, (size, levels), 1)
    spread = place == 0
    across, down = (lax.broadcasted_iota(jnp.int32, (size, size), dim) for dim in (1, 0))
    same = (across < levels) & (down < levels)
    for m in range(1, copies):
        spread = spread | (place == m * levels)
        low, high = m * levels, (m + 1) * levels
        same = same | ((across >= low) & (across < high) & (down >= low) & (down < high))
    spread = jnp.where(spread, 1.0, 0.0).astype(jnp.bfloat16)
    tall = lax.dot_general(spread, vertical, NN, preferred_element_type=jnp.float32).astype(jnp.bfloat16)
    wide = lax.dot_general(tall, spread, NT, preferred_element_type=jnp.float32)
    return jnp.where(same, wide, 0.0).astype(jnp.bfloat16)


def matrices_kernel(groups, row_slots, meta, vertical, after, mixer, upper, lower, starts):
    mixer[...] = block_diagonal(vertical[...], mixer.shape[0] // vertical.shape[0])
    half, lat_pad = upper.shape[0], groups * row_slots
    lat_weights(groups, row_slots, meta, starts, upper, 0, 0)
    lat_weights(groups, row_slots, meta, starts, lower, half, lat_pad - lower.shape[1])


def lat_kernel(groups, masks, meta, mixer, upper, lower, pert, *refs):
    received, (kept, given, field) = refs[:groups], refs[groups:]
    useful = received[0].shape[0]
    for g in range(groups):
        place = (meta[2 * groups] ^ masks[g]) * useful
        field[pl.ds(place, useful), :] = received[g][...].astype(jnp.float32)
    lat_columns(meta[2 * groups + 1] == 1, mixer, pert, upper, lower, field, kept, given)


def sending_order(groups):
    quarter = groups // 4
    far = list(range(2 * quarter, 4 * quarter))
    near = list(range(quarter, 2 * quarter)) + list(range(1, quarter))
    order = []
    for n in range(2 * quarter):
        order += far[n:n + 1] + near[n:n + 1]
    order.remove(far[1])
    return far[:1] + far[1:2] + order[1:]


def per_device(control, perturbation, vertical, lat_counts, lon_counts):
    groups = lax.axis_size("grid")
    shares = lax.axis_size("mem")
    members, levels, row_slots, lon_pad = control.shape
    col_slots, lat_pad = perturbation.shape[2:]
    lanes = members * levels
    vmem = pl.BlockSpec(memory_space=pltpu.VMEM)
    smem = pl.BlockSpec(memory_space=pltpu.SMEM)
    hbm = pl.BlockSpec(memory_space=pl.ANY)
    places = jnp.stack([lax.axis_index("grid"), lax.axis_index("mem") if shares == 2 else 0]).astype(jnp.int32)
    meta = jnp.concatenate([lon_counts, lat_counts, places])
    pert = jnp.transpose(perturbation, (0, 2, 1, 3))

    fields = jnp.transpose(control, (0, 2, 1, 3))

    def lon_filter(kernel, masks, columns, limit, grid, in_specs, *operands):
        return list(pl.pallas_call(
            kernel,
            out_shape=[jax.ShapeDtypeStruct((row_slots * col_slots, lanes), jnp.bfloat16)] * len(masks),
            grid=grid,
            in_specs=[smem, *in_specs],
            out_specs=[vmem] * len(masks),
            scratch_shapes=[
                pltpu.VMEM((len(masks) * round_up(col_slots, 16), columns), jnp.bfloat16),
                pltpu.VMEM((len(masks), row_slots * col_slots, lanes), jnp.float32),
                pltpu.SMEM((groups,), jnp.int32),
            ],
            compiler_params=pltpu.CompilerParams(vmem_limit_bytes=limit),
            name="lon_filter",
        )(*operands))

    def send(mask, value):
        return lax.ppermute(value, "grid", [(g, g ^ mask) for g in range(groups)])

    order = sending_order(groups)
    masks = order + [0]
    width = window_tiles(groups, lon_pad)[1]
    tiles = -(-lon_pad // 128)
    rows = min(FETCH, row_slots)
    windows = [
        pl.BlockSpec(
            (members, rows, levels, 128),
            lambda n, j=j: (0, n, 0, lax.rem(window_begin(groups, lon_pad, masks[0]) + j, tiles)),
        )
        for j in range(width)
    ]
    kernel = functools.partial(first_lon_kernel, groups, masks[:2], row_slots, lon_pad)
    values = lon_filter(
        kernel, masks[:2], width * 128, FIRST_LIMIT, (-(-row_slots // rows),), windows, lon_counts, *[fields] * width
    )
    kernel = functools.partial(lon_kernel, groups, masks[2:])
    values += lon_filter(kernel, masks[2:], lon_pad, LON_LIMIT, (), [vmem, hbm], meta, fields, values[0])
    received = [send(mask, value) if mask else value for mask, value in zip(masks, values)]

    reach = min(lat_reach(groups, row_slots), groups // 2)
    mixer, upper, lower = pl.pallas_call(
        functools.partial(matrices_kernel, groups, row_slots),
        out_shape=[
            jax.ShapeDtypeStruct((2 * lanes, 2 * lanes), jnp.bfloat16),
            jax.ShapeDtypeStruct((lat_pad // 2, lat_pad // 2), jnp.bfloat16),
            jax.ShapeDtypeStruct((lat_pad // 2, lat_pad // 2 + reach * row_slots), jnp.bfloat16),
        ],
        in_specs=[smem, vmem, hbm],
        out_specs=[vmem] * 3,
        scratch_shapes=[pltpu.SMEM((groups,), jnp.int32)],
        compiler_params=pltpu.CompilerParams(vmem_limit_bytes=4 * MIB),
        name="matrices",
    )(meta, vertical, values[-1])

    half = levels // 2
    kept, given = pl.pallas_call(
        functools.partial(lat_kernel, groups, masks),
        out_shape=[
            jax.ShapeDtypeStruct((col_slots, half, lat_pad), jnp.float32),
            jax.ShapeDtypeStruct((col_slots, half, lat_pad), jnp.bfloat16 if shares == 2 else jnp.float32),
        ],
        in_specs=[smem] + [vmem] * (4 + groups),
        out_specs=[vmem] * 2,
        scratch_shapes=[pltpu.VMEM((lat_pad * col_slots, lanes), jnp.float32)],
        compiler_params=pltpu.CompilerParams(vmem_limit_bytes=LAT_LIMIT),
        name="lat_filter",
    )(meta, mixer, upper, lower, pert, *received)
    if shares == 2:
        total = kept + lax.ppermute(given, "mem", [(0, 1), (1, 0)]).astype(jnp.float32)
    else:
        total = lax.psum_scatter(
            jnp.concatenate([kept, given], axis=1), "mem", scatter_dimension=1, tiled=True
        )
    return jnp.transpose(total, (1, 0, 2))


def solution(mesh):
    in_specs = (P("mem", None, "grid", None), P("mem", None, "grid", None), P(), P(), P())
    out_specs = P("mem", "grid", None)
    return jax.shard_map(per_device, mesh=mesh, in_specs=in_specs, out_specs=out_specs, check_vma=False)
```

```python
import functools
import math

import jax
import jax.numpy as jnp
import numpy as np
from jax import lax
from jax.experimental import pallas as pl
from jax.experimental.pallas import tpu as pltpu
from jax.sharding import PartitionSpec as P

LAT = 361
LON = 720
LENGTH = 8
BAND = 48
FAR = 1 << 20
NORM = np.float32(math.sqrt(sum(math.exp(-2.0 * e / LENGTH) for e in range(BAND + 1))))
MIB = 1024 * 1024
FIRST_LIMIT = 60 * MIB
LON_LIMIT = 24 * MIB
LAT_LIMIT = 26 * MIB
FETCH = 12
AHEAD = 3
NT = (((1,), (1,)), ((), ()))
NN = (((1,), (0,)), ((), ()))


def round_up(value, multiple):
    return -(-value // multiple) * multiple


def sums_before(meta, first, starts, groups):
    total = jnp.int32(0)
    for g in range(groups):
        starts[g] = total
        total = total + meta[first + g]


def place_of(meta, first, starts, slab, slots, size):
    inside = (slots >= 0) & (slots < jnp.minimum(meta[first + slab], size))
    return jnp.where(inside, slots + starts[slab], FAR)


def weights(lag, real):
    inside = (lag >= 0) & (lag <= BAND) & real
    value = jnp.exp(lag.astype(jnp.float32) * (-1.0 / LENGTH)) / NORM
    return jnp.where(inside, value, 0.0).astype(jnp.bfloat16)


def lon_weights(groups, masks, meta, me, starts, table, slots, col_slots):
    col_rows = table.shape[0] // len(masks)
    sums_before(meta, 0, starts, groups)
    source = jnp.full_like(slots, FAR)
    for g in range(groups):
        source = jnp.minimum(source, place_of(meta, 0, starts, g, slots - g * col_slots, col_slots))
    own = lax.broadcasted_iota(jnp.int32, (col_rows, 1), 0)
    for n, mask in enumerate(masks):
        slab = me ^ mask
        lag = own + starts[slab] - source
        lag = jnp.where(lag < 0, lag + LON, lag)
        table[n * col_rows:(n + 1) * col_rows, :] = weights(lag, own < meta[slab])


def lon_blocks(masks, row_range, col_slots, rows_of, table, packed, outs):
    lanes = packed.shape[2]
    col_rows = table.shape[0] // len(masks)
    for i in row_range[::2]:
        count = min(2, row_range[-1] + 1 - i)
        field = jnp.concatenate([rows_of(i + r).reshape(lanes, table.shape[1]) for r in range(count)], axis=0)
        smooth = lax.dot_general(table[...], field, NT, preferred_element_type=jnp.float32)
        for n in range(len(masks)):
            for r in range(count):
                packed[n, (i + r) * col_slots:(i + r + 1) * col_slots, :] = smooth[
                    n * col_rows:n * col_rows + col_slots, r * lanes:(r + 1) * lanes
                ]
    for n, out in enumerate(outs):
        out[...] = packed[n, :out.shape[0]].astype(jnp.bfloat16)


def window_tiles(groups, lon_pad):
    col_slots = lon_pad // groups
    tiles = -(-lon_pad // 128)
    reach = -(-(BAND + lon_pad - LON) // col_slots)
    needed = (reach + 2) * col_slots + 127 + tiles * 128 - lon_pad
    return reach, min(-(-needed // 128), tiles)


def window_begin(groups, lon_pad, mask):
    pair = (lax.axis_index("grid") ^ mask) // 2 * 2
    reach, width = window_tiles(groups, lon_pad)
    return lax.rem(pair - reach + groups, groups) * (lon_pad // groups) // 128


def first_lon_kernel(groups, masks, row_slots, lon_pad, counts, *refs):
    width = window_tiles(groups, lon_pad)[1]
    window, outs, (table, packed, starts) = refs[:width], refs[width:-3], refs[-3:]
    col_slots = lon_pad // groups
    tiles = -(-lon_pad // 128)
    begin = window_begin(groups, lon_pad, masks[0])
    lane = lax.broadcasted_iota(jnp.int32, (1, 128), 1)
    slots = [lane + lax.rem(begin + j, tiles) * 128 for j in range(width)]
    step = pl.program_id(0)
    size = window[0].shape[1]

    @pl.when(step == 0)
    def _():
        lon_weights(
            groups, masks, counts, lax.axis_index("grid"), starts, table, jnp.concatenate(slots, axis=1), col_slots
        )

    for n in range(-(-row_slots // size)):
        @pl.when(step == n)
        def _():
            def rows_of(i):
                return jnp.concatenate(
                    [
                        jnp.where(slots[j] < lon_pad, window[j][:, i - n * size].reshape(-1, 128), jnp.bfloat16(0))
                        for j in range(width)
                    ],
                    axis=1,
                )

            last = n * size + size >= row_slots
            lon_blocks(
                masks, range(n * size, row_slots if last else n * size + size), col_slots, rows_of, table, packed,
                outs if last else [],
            )


def lon_kernel(groups, masks, meta, control, *refs):
    outs, (table, packed, starts) = refs[-3 - len(masks):-3], refs[-3:]
    lon_pad = control.shape[3]
    col_slots = lon_pad // groups
    slots = lax.broadcasted_iota(jnp.int32, (1, lon_pad), 1)
    lon_weights(groups, masks, meta, meta[2 * groups], starts, table, slots, col_slots)
    lon_blocks(masks, range(control.shape[1]), col_slots, lambda i: control[:, i], table, packed, outs)


def lat_reach(groups, row_slots):
    return -(-(BAND + groups * row_slots - LAT) // row_slots)


def lat_weights(groups, row_slots, meta, starts, table, first_down, first_across):
    sums_before(meta, groups, starts, groups)
    down_slots = lax.broadcasted_iota(jnp.int32, (table.shape[0], 1), 0) + first_down
    across_slots = lax.broadcasted_iota(jnp.int32, (1, table.shape[1]), 1) + first_across
    down, across = jnp.full_like(down_slots, FAR), jnp.full_like(across_slots, FAR)
    for g in range(groups):
        down = jnp.minimum(down, place_of(meta, groups, starts, g, down_slots - g * row_slots, row_slots))
        across = jnp.minimum(across, place_of(meta, groups, starts, g, across_slots - g * row_slots, row_slots))
    table[...] = weights(down - across, down < FAR)


def lat_columns(second, mixer, pert, upper, lower, field, kept, given):
    columns, half = kept.shape[:2]
    members, _, levels, lat_pad = pert.shape
    lanes = members * levels

    def filtered(c):
        halves = []
        for table, first in ((upper, 0), (lower, lat_pad - lower.shape[1])):
            part = jnp.concatenate(
                [
                    field[pl.ds(first * columns + c + r, table.shape[1], columns), :].astype(jnp.bfloat16)
                    for r in range(2)
                ],
                axis=1,
            )
            halves.append(lax.dot_general(table[...], part, NN, preferred_element_type=jnp.float32))
        return jnp.concatenate(halves, axis=0).astype(jnp.bfloat16)

    def finish(c, smooth):
        pair = lax.dot_general(mixer[...], smooth, NT, preferred_element_type=jnp.float32)
        for r in range(2):
            mixed = pair[r * lanes:(r + 1) * lanes]
            total = mixed[:levels] * pert[0, c + r].astype(jnp.float32)
            for m in range(1, members):
                total = total + mixed[m * levels:(m + 1) * levels] * pert[m, c + r].astype(jnp.float32)
            kept[c + r] = jnp.where(second, total[half:], total[:half])
            given[c + r] = jnp.where(second, total[:half], total[half:]).astype(given.dtype)

    ahead = []
    for c in range(0, columns, 2):
        ahead.append((c, filtered(c)))
        if len(ahead) > AHEAD:
            finish(*ahead.pop(0))
    for item in ahead:
        finish(*item)


def block_diagonal(vertical, copies):
    levels = vertical.shape[0]
    size = copies * levels
    place = lax.broadcasted_iota(jnp.int32, (size, levels), 0) - lax.broadcasted_iota(jnp.int32, (size, levels), 1)
    spread = place == 0
    across, down = (lax.broadcasted_iota(jnp.int32, (size, size), dim) for dim in (1, 0))
    same = (across < levels) & (down < levels)
    for m in range(1, copies):
        spread = spread | (place == m * levels)
        low, high = m * levels, (m + 1) * levels
        same = same | ((across >= low) & (across < high) & (down >= low) & (down < high))
    spread = jnp.where(spread, 1.0, 0.0).astype(jnp.bfloat16)
    tall = lax.dot_general(spread, vertical, NN, preferred_element_type=jnp.float32).astype(jnp.bfloat16)
    wide = lax.dot_general(tall, spread, NT, preferred_element_type=jnp.float32)
    return jnp.where(same, wide, 0.0).astype(jnp.bfloat16)


def matrices_kernel(groups, row_slots, meta, vertical, after, mixer, upper, lower, starts):
    mixer[...] = block_diagonal(vertical[...], mixer.shape[0] // vertical.shape[0])
    half, lat_pad = upper.shape[0], groups * row_slots
    lat_weights(groups, row_slots, meta, starts, upper, 0, 0)
    lat_weights(groups, row_slots, meta, starts, lower, half, lat_pad - lower.shape[1])


def lat_kernel(groups, masks, meta, mixer, upper, lower, pert, *refs):
    received, (kept, given, field) = refs[:groups], refs[groups:]
    useful = received[0].shape[0]
    for g in range(groups):
        place = (meta[2 * groups] ^ masks[g]) * useful
        field[pl.ds(place, useful), :] = received[g][...].astype(jnp.float32)
    lat_columns(meta[2 * groups + 1] == 1, mixer, pert, upper, lower, field, kept, given)


def sending_order(groups):
    quarter = groups // 4
    far = list(range(2 * quarter, 4 * quarter))
    near = list(range(quarter, 2 * quarter)) + list(range(1, quarter))
    order = []
    for n in range(2 * quarter):
        order += far[n:n + 1] + near[n:n + 1]
    order.remove(far[1])
    return far[:1] + far[1:2] + order[1:]


def per_device(control, perturbation, vertical, lat_counts, lon_counts):
    groups = lax.axis_size("grid")
    shares = lax.axis_size("mem")
    members, levels, row_slots, lon_pad = control.shape
    col_slots, lat_pad = perturbation.shape[2:]
    lanes = members * levels
    vmem = pl.BlockSpec(memory_space=pltpu.VMEM)
    smem = pl.BlockSpec(memory_space=pltpu.SMEM)
    hbm = pl.BlockSpec(memory_space=pl.ANY)
    places = jnp.stack([lax.axis_index("grid"), lax.axis_index("mem") if shares == 2 else 0]).astype(jnp.int32)
    meta = jnp.concatenate([lon_counts, lat_counts, places])
    pert = jnp.transpose(perturbation, (0, 2, 1, 3))

    fields = jnp.transpose(control, (0, 2, 1, 3))

    def lon_filter(kernel, masks, columns, limit, grid, in_specs, *operands):
        return list(pl.pallas_call(
            kernel,
            out_shape=[jax.ShapeDtypeStruct((row_slots * col_slots, lanes), jnp.bfloat16)] * len(masks),
            grid=grid,
            in_specs=[smem, *in_specs],
            out_specs=[vmem] * len(masks),
            scratch_shapes=[
                pltpu.VMEM((len(masks) * round_up(col_slots, 16), columns), jnp.bfloat16),
                pltpu.VMEM((len(masks), round_up(row_slots * col_slots, 8) + 8, lanes), jnp.float32),
                pltpu.SMEM((groups,), jnp.int32),
            ],
            compiler_params=pltpu.CompilerParams(vmem_limit_bytes=limit),
            name="lon_filter",
        )(*operands))

    def send(mask, value):
        return lax.ppermute(value, "grid", [(g, g ^ mask) for g in range(groups)])

    order = sending_order(groups)
    masks = order + [0]
    width = window_tiles(groups, lon_pad)[1]
    tiles = -(-lon_pad // 128)
    rows = min(FETCH, row_slots)
    windows = [
        pl.BlockSpec(
            (members, rows, levels, 128),
            lambda n, j=j: (0, n, 0, lax.rem(window_begin(groups, lon_pad, masks[0]) + j, tiles)),
        )
        for j in range(width)
    ]
    kernel = functools.partial(first_lon_kernel, groups, masks[:2], row_slots, lon_pad)
    values = lon_filter(
        kernel, masks[:2], width * 128, FIRST_LIMIT, (-(-row_slots // rows),), windows, lon_counts, *[fields] * width
    )
    kernel = functools.partial(lon_kernel, groups, masks[2:])
    values += lon_filter(kernel, masks[2:], lon_pad, LON_LIMIT, (), [vmem, hbm], meta, fields, values[0])
    received = [send(mask, value) if mask else value for mask, value in zip(masks, values)]

    reach = min(lat_reach(groups, row_slots), groups // 2)
    mixer, upper, lower = pl.pallas_call(
        functools.partial(matrices_kernel, groups, row_slots),
        out_shape=[
            jax.ShapeDtypeStruct((2 * lanes, 2 * lanes), jnp.bfloat16),
            jax.ShapeDtypeStruct((lat_pad // 2, lat_pad // 2), jnp.bfloat16),
            jax.ShapeDtypeStruct((lat_pad // 2, lat_pad // 2 + reach * row_slots), jnp.bfloat16),
        ],
        in_specs=[smem, vmem, hbm],
        out_specs=[vmem] * 3,
        scratch_shapes=[pltpu.SMEM((groups,), jnp.int32)],
        compiler_params=pltpu.CompilerParams(vmem_limit_bytes=4 * MIB),
        name="matrices",
    )(meta, vertical, values[-1])

    half = levels // 2
    kept, given = pl.pallas_call(
        functools.partial(lat_kernel, groups, masks),
        out_shape=[
            jax.ShapeDtypeStruct((col_slots, half, lat_pad), jnp.float32),
            jax.ShapeDtypeStruct((col_slots, half, lat_pad), jnp.bfloat16 if shares == 2 else jnp.float32),
        ],
        in_specs=[smem] + [vmem] * (4 + groups),
        out_specs=[vmem] * 2,
        scratch_shapes=[pltpu.VMEM(((lat_pad + 8) * col_slots, lanes), jnp.float32)],
        compiler_params=pltpu.CompilerParams(vmem_limit_bytes=LAT_LIMIT),
        name="lat_filter",
    )(meta, mixer, upper, lower, pert, *received)
    if shares == 2:
        total = kept + lax.ppermute(given, "mem", [(0, 1), (1, 0)]).astype(jnp.float32)
    else:
        total = lax.psum_scatter(
            jnp.concatenate([kept, given], axis=1), "mem", scatter_dimension=1, tiled=True
        )
    return jnp.transpose(total, (1, 0, 2))


def solution(mesh):
    in_specs = (P("mem", None, "grid", None), P("mem", None, "grid", None), P(), P(), P())
    out_specs = P("mem", "grid", None)
    return jax.shard_map(per_device, mesh=mesh, in_specs=in_specs, out_specs=out_specs, check_vma=False)
```

```python
import functools
import math

import jax
import jax.numpy as jnp
import numpy as np
from jax import lax
from jax.experimental import pallas as pl
from jax.experimental.pallas import tpu as pltpu
from jax.sharding import PartitionSpec as P

LAT = 361
LON = 720
LENGTH = 8
BAND = 48
FAR = 1 << 20
NORM = np.float32(math.sqrt(sum(math.exp(-2.0 * e / LENGTH) for e in range(BAND + 1))))
MIB = 1024 * 1024
FIRST_LIMIT = 60 * MIB
LON_LIMIT = 24 * MIB
LAT_LIMIT = 26 * MIB
FETCH = 24
AHEAD = 3
NT = (((1,), (1,)), ((), ()))
NN = (((1,), (0,)), ((), ()))


def round_up(value, multiple):
    return -(-value // multiple) * multiple


def sums_before(meta, first, starts, groups):
    total = jnp.int32(0)
    for g in range(groups):
        starts[g] = total
        total = total + meta[first + g]


def place_of(meta, first, starts, slab, slots, size):
    inside = (slots >= 0) & (slots < jnp.minimum(meta[first + slab], size))
    return jnp.where(inside, slots + starts[slab], FAR)


def weights(lag, real):
    inside = (lag >= 0) & (lag <= BAND) & real
    value = jnp.exp(lag.astype(jnp.float32) * (-1.0 / LENGTH)) / NORM
    return jnp.where(inside, value, 0.0).astype(jnp.bfloat16)


def lon_weights(groups, masks, meta, me, starts, table, slots, col_slots):
    col_rows = table.shape[0] // len(masks)
    sums_before(meta, 0, starts, groups)
    source = jnp.full_like(slots, FAR)
    for g in range(groups):
        source = jnp.minimum(source, place_of(meta, 0, starts, g, slots - g * col_slots, col_slots))
    own = lax.broadcasted_iota(jnp.int32, (col_rows, 1), 0)
    for n, mask in enumerate(masks):
        slab = me ^ mask
        lag = own + starts[slab] - source
        lag = jnp.where(lag < 0, lag + LON, lag)
        table[n * col_rows:(n + 1) * col_rows, :] = weights(lag, own < meta[slab])


def lon_blocks(masks, row_range, col_slots, rows_of, table, packed, outs):
    lanes = packed.shape[2]
    col_rows = table.shape[0] // len(masks)
    for i in row_range[::2]:
        count = min(2, row_range[-1] + 1 - i)
        field = jnp.concatenate([rows_of(i + r).reshape(lanes, table.shape[1]) for r in range(count)], axis=0)
        smooth = lax.dot_general(table[...], field, NT, preferred_element_type=jnp.float32)
        for n in range(len(masks)):
            for r in range(count):
                packed[n, (i + r) * col_slots:(i + r + 1) * col_slots, :] = smooth[
                    n * col_rows:n * col_rows + col_slots, r * lanes:(r + 1) * lanes
                ]
    for n, out in enumerate(outs):
        out[...] = packed[n, :out.shape[0]].astype(jnp.bfloat16)


def window_tiles(groups, lon_pad):
    col_slots = lon_pad // groups
    tiles = -(-lon_pad // 128)
    reach = -(-(BAND + lon_pad - LON) // col_slots)
    needed = (reach + 2) * col_slots + 127 + tiles * 128 - lon_pad
    return reach, min(-(-needed // 128), tiles)


def window_begin(groups, lon_pad, mask):
    pair = (lax.axis_index("grid") ^ mask) // 2 * 2
    reach, width = window_tiles(groups, lon_pad)
    return lax.rem(pair - reach + groups, groups) * (lon_pad // groups) // 128


def first_lon_kernel(groups, masks, row_slots, lon_pad, counts, *refs):
    width = window_tiles(groups, lon_pad)[1]
    window, outs, (table, packed, starts) = refs[:width], refs[width:-3], refs[-3:]
    col_slots = lon_pad // groups
    tiles = -(-lon_pad // 128)
    begin = window_begin(groups, lon_pad, masks[0])
    lane = lax.broadcasted_iota(jnp.int32, (1, 128), 1)
    slots = [lane + lax.rem(begin + j, tiles) * 128 for j in range(width)]
    step = pl.program_id(0)
    size = window[0].shape[1]

    @pl.when(step == 0)
    def _():
        lon_weights(
            groups, masks, counts, lax.axis_index("grid"), starts, table, jnp.concatenate(slots, axis=1), col_slots
        )

    for n in range(-(-row_slots // size)):
        @pl.when(step == n)
        def _():
            def rows_of(i):
                return jnp.concatenate(
                    [
                        jnp.where(slots[j] < lon_pad, window[j][:, i - n * size].reshape(-1, 128), jnp.bfloat16(0))
                        for j in range(width)
                    ],
                    axis=1,
                )

            last = n * size + size >= row_slots
            lon_blocks(
                masks, range(n * size, row_slots if last else n * size + size), col_slots, rows_of, table, packed,
                outs if last else [],
            )


def lon_kernel(groups, masks, meta, control, *refs):
    outs, (table, packed, starts) = refs[-3 - len(masks):-3], refs[-3:]
    lon_pad = control.shape[3]
    col_slots = lon_pad // groups
    slots = lax.broadcasted_iota(jnp.int32, (1, lon_pad), 1)
    lon_weights(groups, masks, meta, meta[2 * groups], starts, table, slots, col_slots)
    lon_blocks(masks, range(control.shape[1]), col_slots, lambda i: control[:, i], table, packed, outs)


def lat_reach(groups, row_slots):
    return -(-(BAND + groups * row_slots - LAT) // row_slots)


def lat_weights(groups, row_slots, meta, starts, table, first_down, first_across):
    sums_before(meta, groups, starts, groups)
    down_slots = lax.broadcasted_iota(jnp.int32, (table.shape[0], 1), 0) + first_down
    across_slots = lax.broadcasted_iota(jnp.int32, (1, table.shape[1]), 1) + first_across
    down, across = jnp.full_like(down_slots, FAR), jnp.full_like(across_slots, FAR)
    for g in range(groups):
        down = jnp.minimum(down, place_of(meta, groups, starts, g, down_slots - g * row_slots, row_slots))
        across = jnp.minimum(across, place_of(meta, groups, starts, g, across_slots - g * row_slots, row_slots))
    table[...] = weights(down - across, down < FAR)


def lat_columns(second, mixer, pert, upper, lower, field, kept, given):
    columns, half = kept.shape[:2]
    members, _, levels, lat_pad = pert.shape
    lanes = members * levels

    def filtered(c):
        halves = []
        for table, first in ((upper, 0), (lower, lat_pad - lower.shape[1])):
            part = jnp.concatenate(
                [
                    field[pl.ds(first * columns + c + r, table.shape[1], columns), :].astype(jnp.bfloat16)
                    for r in range(2)
                ],
                axis=1,
            )
            halves.append(lax.dot_general(table[...], part, NN, preferred_element_type=jnp.float32))
        return jnp.concatenate(halves, axis=0).astype(jnp.bfloat16)

    def finish(c, smooth):
        pair = lax.dot_general(mixer[...], smooth, NT, preferred_element_type=jnp.float32)
        for r in range(2):
            mixed = pair[r * lanes:(r + 1) * lanes]
            total = mixed[:levels] * pert[0, c + r].astype(jnp.float32)
            for m in range(1, members):
                total = total + mixed[m * levels:(m + 1) * levels] * pert[m, c + r].astype(jnp.float32)
            kept[c + r] = jnp.where(second, total[half:], total[:half])
            given[c + r] = jnp.where(second, total[:half], total[half:]).astype(given.dtype)

    ahead = []
    for c in range(0, columns, 2):
        ahead.append((c, filtered(c)))
        if len(ahead) > AHEAD:
            finish(*ahead.pop(0))
    for item in ahead:
        finish(*item)


def block_diagonal(vertical, copies):
    levels = vertical.shape[0]
    size = copies * levels
    place = lax.broadcasted_iota(jnp.int32, (size, levels), 0) - lax.broadcasted_iota(jnp.int32, (size, levels), 1)
    spread = place == 0
    across, down = (lax.broadcasted_iota(jnp.int32, (size, size), dim) for dim in (1, 0))
    same = (across < levels) & (down < levels)
    for m in range(1, copies):
        spread = spread | (place == m * levels)
        low, high = m * levels, (m + 1) * levels
        same = same | ((across >= low) & (across < high) & (down >= low) & (down < high))
    spread = jnp.where(spread, 1.0, 0.0).astype(jnp.bfloat16)
    tall = lax.dot_general(spread, vertical, NN, preferred_element_type=jnp.float32).astype(jnp.bfloat16)
    wide = lax.dot_general(tall, spread, NT, preferred_element_type=jnp.float32)
    return jnp.where(same, wide, 0.0).astype(jnp.bfloat16)


def matrices_kernel(groups, row_slots, meta, vertical, after, mixer, upper, lower, starts):
    mixer[...] = block_diagonal(vertical[...], mixer.shape[0] // vertical.shape[0])
    half, lat_pad = upper.shape[0], groups * row_slots
    lat_weights(groups, row_slots, meta, starts, upper, 0, 0)
    lat_weights(groups, row_slots, meta, starts, lower, half, lat_pad - lower.shape[1])


def lat_kernel(groups, masks, meta, mixer, upper, lower, pert, *refs):
    received, (kept, given, field) = refs[:groups], refs[groups:]
    useful = received[0].shape[0]
    for g in range(groups):
        place = (meta[2 * groups] ^ masks[g]) * useful
        field[pl.ds(place, useful), :] = received[g][...].astype(jnp.float32)
    lat_columns(meta[2 * groups + 1] == 1, mixer, pert, upper, lower, field, kept, given)


def sending_order(groups):
    quarter = groups // 4
    far = list(range(2 * quarter, 4 * quarter))
    near = list(range(quarter, 2 * quarter)) + list(range(1, quarter))
    order = []
    for n in range(2 * quarter):
        order += far[n:n + 1] + near[n:n + 1]
    order.remove(far[1])
    return far[:1] + far[1:2] + order[1:]


def per_device(control, perturbation, vertical, lat_counts, lon_counts):
    groups = lax.axis_size("grid")
    shares = lax.axis_size("mem")
    members, levels, row_slots, lon_pad = control.shape
    col_slots, lat_pad = perturbation.shape[2:]
    lanes = members * levels
    vmem = pl.BlockSpec(memory_space=pltpu.VMEM)
    smem = pl.BlockSpec(memory_space=pltpu.SMEM)
    hbm = pl.BlockSpec(memory_space=pl.ANY)
    places = jnp.stack([lax.axis_index("grid"), lax.axis_index("mem") if shares == 2 else 0]).astype(jnp.int32)
    meta = jnp.concatenate([lon_counts, lat_counts, places])
    pert = jnp.transpose(perturbation, (0, 2, 1, 3))

    fields = jnp.transpose(control, (0, 2, 1, 3))

    def lon_filter(kernel, masks, columns, limit, grid, in_specs, *operands):
        return list(pl.pallas_call(
            kernel,
            out_shape=[jax.ShapeDtypeStruct((row_slots * col_slots, lanes), jnp.bfloat16)] * len(masks),
            grid=grid,
            in_specs=[smem, *in_specs],
            out_specs=[vmem] * len(masks),
            scratch_shapes=[
                pltpu.VMEM((len(masks) * round_up(col_slots, 16), columns), jnp.bfloat16),
                pltpu.VMEM((len(masks), round_up(row_slots * col_slots, 8) + 8, lanes), jnp.float32),
                pltpu.SMEM((groups,), jnp.int32),
            ],
            compiler_params=pltpu.CompilerParams(vmem_limit_bytes=limit),
            name="lon_filter",
        )(*operands))

    def send(mask, value):
        return lax.ppermute(value, "grid", [(g, g ^ mask) for g in range(groups)])

    order = sending_order(groups)
    masks = order + [0]
    width = window_tiles(groups, lon_pad)[1]
    tiles = -(-lon_pad // 128)
    rows = min(FETCH, row_slots)
    windows = [
        pl.BlockSpec(
            (members, rows, levels, 128),
            lambda n, j=j: (0, n, 0, lax.rem(window_begin(groups, lon_pad, masks[0]) + j, tiles)),
        )
        for j in range(width)
    ]
    kernel = functools.partial(first_lon_kernel, groups, masks[:2], row_slots, lon_pad)
    values = lon_filter(
        kernel, masks[:2], width * 128, FIRST_LIMIT, (-(-row_slots // rows),), windows, lon_counts, *[fields] * width
    )
    kernel = functools.partial(lon_kernel, groups, masks[2:])
    values += lon_filter(kernel, masks[2:], lon_pad, LON_LIMIT, (), [vmem, hbm], meta, fields, values[0])
    received = [send(mask, value) if mask else value for mask, value in zip(masks, values)]

    reach = min(lat_reach(groups, row_slots), groups // 2)
    mixer, upper, lower = pl.pallas_call(
        functools.partial(matrices_kernel, groups, row_slots),
        out_shape=[
            jax.ShapeDtypeStruct((2 * lanes, 2 * lanes), jnp.bfloat16),
            jax.ShapeDtypeStruct((lat_pad // 2, lat_pad // 2), jnp.bfloat16),
            jax.ShapeDtypeStruct((lat_pad // 2, lat_pad // 2 + reach * row_slots), jnp.bfloat16),
        ],
        in_specs=[smem, vmem, hbm],
        out_specs=[vmem] * 3,
        scratch_shapes=[pltpu.SMEM((groups,), jnp.int32)],
        compiler_params=pltpu.CompilerParams(vmem_limit_bytes=4 * MIB),
        name="matrices",
    )(meta, vertical, values[-1])

    half = levels // 2
    kept, given = pl.pallas_call(
        functools.partial(lat_kernel, groups, masks),
        out_shape=[
            jax.ShapeDtypeStruct((col_slots, half, lat_pad), jnp.float32),
            jax.ShapeDtypeStruct((col_slots, half, lat_pad), jnp.bfloat16 if shares == 2 else jnp.float32),
        ],
        in_specs=[smem] + [vmem] * (4 + groups),
        out_specs=[vmem] * 2,
        scratch_shapes=[pltpu.VMEM(((lat_pad + 8) * col_slots, lanes), jnp.float32)],
        compiler_params=pltpu.CompilerParams(vmem_limit_bytes=LAT_LIMIT),
        name="lat_filter",
    )(meta, mixer, upper, lower, pert, *received)
    if shares == 2:
        total = kept + lax.ppermute(given, "mem", [(0, 1), (1, 0)]).astype(jnp.float32)
    else:
        total = lax.psum_scatter(
            jnp.concatenate([kept, given], axis=1), "mem", scatter_dimension=1, tiled=True
        )
    return jnp.transpose(total, (1, 0, 2))


def solution(mesh):
    in_specs = (P("mem", None, "grid", None), P("mem", None, "grid", None), P(), P(), P())
    out_specs = P("mem", "grid", None)
    return jax.shard_map(per_device, mesh=mesh, in_specs=in_specs, out_specs=out_specs, check_vma=False)
```
